32 devices in a mesh: lat: 4 (over x, core), lon: 8 (over z, y).
Axes of the slice: x: 2, y: 2, z: 4, core: 2. Of those that a mesh axis runs over, the one named last changes fastest.
Arguments:
- fields: bfloat16 [4, 16, 72, 1024], P(None, 'lat', 'lon'), may hold values from -6 to 6
- conv_first: float32 [9, 1024], replicated, may hold values from -2 to 2
- w_qkv: bfloat16 [1024, 3072], replicated, may hold values from -2 to 2
- w_out: bfloat16 [1024, 1024], replicated, may hold values from -0.1875 to 0.1875
- conv_second: float32 [9, 1024], replicated, may hold values from -2 to 2
- key_list: int32 [4, 8, 8], P('lat', 'lon'), may hold values from 0 to 7, as said below
- key_count: int32 [4, 8], P('lat', 'lon'), may hold values from 1 to 8, as said below
Outputs:
- attended: bfloat16 [4, 16, 72, 1024], P(None, 'lat', 'lon')
- mixed: bfloat16 [4, 16, 72, 1024], P(None, 'lat', 'lon')
The draws below stay inside these ranges and needn't reach their ends.
Inputs may be any that keep to these rules, and one draw needn't show every extreme that they name: Entry 0 of key_list[p, q] is q; entries 1 to key_count[p, q] - 1 are distinct longitude band indices other than q; the remaining entries are q. key_count[p, q] is 8 in the first and the last latitude band.
All inputs are finite; a program needn't handle non-finite values.
Results may differ from the reference program's by a relative error of at most 0.034.
Values may be sent and summed in bfloat16 or wider, within the bound.
No kernel may reach another device: no remote copies, remote signals or barrier semaphores. Data moves between devices by JAX's collectives and lax.ppermute only.
A program may use at most 128 MiB of HBM per device.

```python
import jax
import jax.numpy as jnp
from jax import lax

D = 1024
HEADS = 16
HEAD = 64
LEVELS = 4
ROWS_DEV = 4
COLS_DEV = 9
TOK_DEV = 144
LAT_BLOCKS = 4
LON_BLOCKS = 8
LAT_ROWS = 16
LON_COLS = 72


def draw_fields(key, part):
    values = jax.random.normal(key, (LEVELS, LAT_ROWS, LON_COLS, D), jnp.float32)
    return jnp.clip(values, -6.0, 6.0).astype(jnp.bfloat16)


def draw_w_qkv(key, part):
    factor = D ** (-0.5)
    w_query = jax.random.normal(jax.random.fold_in(key, 1), (D, D), jnp.float32) * factor
    w_key = jax.random.normal(jax.random.fold_in(key, 2), (D, D), jnp.float32) * factor
    w_value = jax.random.normal(jax.random.fold_in(key, 3), (D, D), jnp.float32) * factor
    query_out = w_query * 1.6
    key_out = w_key * 1.6
    return jnp.concatenate([query_out, key_out, w_value], axis=1).astype(jnp.bfloat16)


def teleconnections(key):
    band_index = jnp.arange(LAT_BLOCKS, dtype=jnp.int32)[:, None]
    distance = jnp.minimum(band_index, LAT_BLOCKS - 1 - band_index)
    half_bands = max(1, LAT_BLOCKS // 2)
    ceiling = jnp.clip((LON_BLOCKS * (half_bands - distance) + half_bands - 1) // half_bands, 2, LON_BLOCKS)
    ceiling = jnp.broadcast_to(ceiling, (LAT_BLOCKS, LON_BLOCKS))
    counts = jax.random.randint(jax.random.fold_in(key, 11), (LAT_BLOCKS, LON_BLOCKS), 1, ceiling + 1)
    counts = jnp.where(jnp.broadcast_to(distance, (LAT_BLOCKS, LON_BLOCKS)) == 0, LON_BLOCKS, counts).astype(jnp.int32)
    scores = jax.random.randint(jax.random.fold_in(key, 12), (LAT_BLOCKS, LON_BLOCKS, LON_BLOCKS - 1), 0, 1 << 20)
    scores = scores * (LON_BLOCKS - 1) + jnp.arange(LON_BLOCKS - 1, dtype=jnp.int32)
    order = jnp.argsort(scores, axis=-1, stable=True).astype(jnp.int32)
    own = jnp.broadcast_to(jnp.arange(LON_BLOCKS, dtype=jnp.int32)[None, :, None], (LAT_BLOCKS, LON_BLOCKS, 1))
    others = (own + order + 1) % LON_BLOCKS
    listed = jnp.concatenate([own, others], axis=-1)
    slot_index = jnp.arange(LON_BLOCKS, dtype=jnp.int32)
    listed = jnp.where(slot_index[None, None, :] < counts[..., None], listed, own)
    return (listed.astype(jnp.int32), counts)


def draw_key_list(key, part):
    return teleconnections(key)[0]


def draw_key_count(key, part):
    return teleconnections(key)[1]


def centred(own_key, shape, spread, bound, kind=jnp.bfloat16):
    entries = jax.random.normal(own_key, shape, jnp.float32) * spread
    return jnp.minimum(jnp.maximum(entries, -bound), bound).astype(kind)


def setup_inputs(seed: int = 0) -> dict:
    arg_keys = jax.random.split(jax.random.key(seed), 8)
    fields = draw_fields(jax.random.fold_in(arg_keys[7], 71), 0)
    conv_first = centred(arg_keys[1], (9, D), 9 ** -0.5, 2.0, jnp.float32)
    w_qkv = draw_w_qkv(jax.random.fold_in(arg_keys[7], 71), 0)
    w_out = centred(arg_keys[3], (D, D), D ** -0.5, 0.1875)
    conv_second = centred(arg_keys[4], (9, D), 9 ** -0.5, 2.0, jnp.float32)
    key_list = draw_key_list(jax.random.fold_in(arg_keys[7], 71), 0)
    key_count = draw_key_count(jax.random.fold_in(arg_keys[7], 71), 0)
    return dict(fields=fields, conv_first=conv_first, w_qkv=w_qkv, w_out=w_out, conv_second=conv_second, key_list=key_list, key_count=key_count)


NEG_FILL = -1e+30
EPSILON = 1e-05

def depthwise(field, weights):
    row_count = field.shape[1]
    column_count = field.shape[2]
    widened = field.astype(jnp.float32)
    widened = jnp.concatenate([widened[:, :, -1:], widened, widened[:, :, :1]], axis=2)
    widened = jnp.pad(widened, ((0, 0), (1, 1), (0, 0), (0, 0)))
    result = jnp.zeros(field.shape, jnp.float32)
    for offset_lat in range(3):
        for offset_lon in range(3):
            result = result + weights[3 * offset_lat + offset_lon] * widened[:, offset_lat:offset_lat + row_count, offset_lon:offset_lon + column_count]
    return result

def to_blocks(array):
    shaped = array.reshape(LEVELS, LAT_BLOCKS, ROWS_DEV, LON_BLOCKS, COLS_DEV, array.shape[-1])
    return shaped.transpose(1, 3, 0, 2, 4, 5).reshape(LAT_BLOCKS, LON_BLOCKS, TOK_DEV, array.shape[-1])

def attend_all(query, keyvals, valid):
    queries = query.astype(jnp.float32).reshape(TOK_DEV, HEADS, HEAD)
    keys_part = keyvals[:, :D].astype(jnp.float32).reshape(-1, HEADS, HEAD)
    values_part = keyvals[:, D:].astype(jnp.float32).reshape(-1, HEADS, HEAD)
    scores = jnp.einsum('qhd,khd->qhk', queries, keys_part) * HEAD ** (-0.5)
    scores = jnp.where(valid[None, None, :], scores, NEG_FILL)
    highest = lax.optimization_barrier(jnp.max(scores, axis=-1, keepdims=True))
    weights = jnp.where(valid[None, None, :], jnp.exp(scores - highest), 0.0)
    summed = lax.optimization_barrier(jnp.sum(weights, axis=-1))
    rounded = lax.optimization_barrier(weights.astype(jnp.bfloat16)).astype(jnp.float32)
    result = jnp.einsum('qhk,khd->qhd', rounded, values_part) / summed[..., None]
    return result.reshape(TOK_DEV, D).astype(jnp.bfloat16)

def reference(fields, conv_first, w_qkv, w_out, conv_second, key_list, key_count):
    stream = (fields.astype(jnp.float32) + depthwise(fields, conv_first)).astype(jnp.bfloat16)
    flat = stream.reshape(-1, D).astype(jnp.float32)
    normed = (flat * lax.rsqrt(lax.optimization_barrier(jnp.mean(flat * flat, axis=-1, keepdims=True)) + EPSILON)).astype(jnp.bfloat16)
    packed = jnp.dot(normed, w_qkv, preferred_element_type=jnp.float32).astype(jnp.bfloat16)
    blocks = to_blocks(packed)
    queries = blocks[..., :D]
    keyvals = blocks[..., D:]
    slot_index = jnp.arange(LON_BLOCKS, dtype=jnp.int32)

    def one_block(index):
        lat_band = index // LON_BLOCKS
        lon_band = index % LON_BLOCKS
        query = queries[lat_band, lon_band]
        band = keyvals[lat_band].reshape(LON_BLOCKS * TOK_DEV, 2 * D)
        upper = keyvals[jnp.maximum(lat_band - 1, 0), lon_band]
        lower = keyvals[jnp.minimum(lat_band + 1, LAT_BLOCKS - 1), lon_band]
        keys_all = jnp.concatenate([band, upper, lower], axis=0)
        listed = key_list[lat_band, lon_band]
        used = slot_index < key_count[lat_band, lon_band]
        linked = jnp.any((listed[None, :] == slot_index[:, None]) & used[None, :], axis=1)
        valid = jnp.concatenate([jnp.repeat(linked, TOK_DEV), jnp.full((TOK_DEV,), lat_band > 0), jnp.full((TOK_DEV,), lat_band < LAT_BLOCKS - 1)])
        return attend_all(query, keys_all, valid)
    outputs = lax.map(one_block, jnp.arange(LAT_BLOCKS * LON_BLOCKS, dtype=jnp.int32))
    outputs = outputs.reshape(LAT_BLOCKS, LON_BLOCKS, LEVELS, ROWS_DEV, COLS_DEV, D)
    attended = outputs.transpose(2, 0, 3, 1, 4, 5).reshape(LEVELS, LAT_ROWS, LON_COLS, D)
    projected = jnp.dot(attended.reshape(-1, D), w_out, preferred_element_type=jnp.float32)
    after = (flat_stream_f32(stream) + projected).astype(jnp.bfloat16).reshape(fields.shape)
    mixed = (after.astype(jnp.float32) + depthwise(after, conv_second)).astype(jnp.bfloat16)
    return (attended, mixed)

def flat_stream_f32(stream):
    return stream.reshape(-1, D).astype(jnp.float32)
```

```python
import functools

import jax
import jax.numpy as jnp
import numpy as np
from jax import lax
from jax.experimental import pallas as pl
from jax.experimental.pallas import tpu as pltpu
from jax.sharding import PartitionSpec as P

HEADS = 16
EPSILON = 1e-05
MASKED = -1e30
LANES = 128
GROUP = 256
F32 = jnp.float32
BF16 = jnp.bfloat16
VMEM_LIMIT = 40 * 1024 * 1024


def ring_order(count):
    columns = 1
    while columns * columns * 4 <= count:
        columns *= 2
    rows = count // columns
    order = [z * columns for z in range(rows)]
    for turn, z in enumerate(range(rows - 1, -1, -1)):
        ys = list(range(1, columns))
        if turn % 2:
            ys.reverse()
        order += [z * columns + y for y in ys]
    return order


def shift(x, axis, by):
    size = lax.axis_size(axis)
    return lax.ppermute(x, axis, [(i, (i + by) % size) for i in range(size)])


def spec(memory_space):
    return pl.BlockSpec(memory_space=memory_space)


def conv_taps(ext, weights_ref, level, row, columns):
    total = None
    for a in range(3):
        for b in range(3):
            term = weights_ref[3 * a + b : 3 * a + b + 1, :] * ext[level, row + a, b : b + columns, :]
            total = term if total is None else total + term
    return total


def fill_ext(ext, center_ref, north_ref, south_ref, west_ref, east_ref, inside_ref):
    levels, rows, columns, width = center_ref.shape
    has_north = (inside_ref[0] > 0).astype(F32)
    has_south = (inside_ref[1] > 0).astype(F32)
    for level in range(levels):
        ext[level, 0, 1 : columns + 1, :] = north_ref[level].astype(F32) * has_north
        ext[level, rows + 1, 1 : columns + 1, :] = south_ref[level].astype(F32) * has_south
        for row in range(rows):
            ext[level, row + 1, 1 : columns + 1, :] = center_ref[level, row].astype(F32)
    west = west_ref[...].astype(F32)
    east = east_ref[...].astype(F32)
    for level in range(levels):
        for row in range(rows + 2):
            at = level * (rows + 2) + row
            ext[level, row, 0:1, :] = west[at : at + 1]
            ext[level, row, columns + 1 : columns + 2, :] = east[at : at + 1]


def first_kernel(inside_ref, fields_ref, north_ref, south_ref, west_ref, east_ref, weights_ref, stream_ref, normed_ref, ext, dense):
    levels, rows, columns, width = fields_ref.shape
    fill_ext(ext, fields_ref, north_ref, south_ref, west_ref, east_ref, inside_ref)
    for level in range(levels):
        for row in range(rows):
            total = conv_taps(ext, weights_ref, level, row, columns)
            value = ext[level, row + 1, 1 : columns + 1, :] + total
            at = (level * rows + row) * columns
            dense[at : at + columns, :] = value
    stream = dense[...].astype(BF16)
    stream_ref[...] = stream
    wide = stream.astype(F32)
    mean = jnp.mean(wide * wide, axis=-1, keepdims=True)
    normed_ref[...] = (wide * lax.rsqrt(mean + EPSILON)).astype(BF16)


def second_kernel(inside_ref, after_ref, north_ref, south_ref, west_ref, east_ref, weights_ref, mixed_ref, ext):
    levels, rows, columns, width = after_ref.shape
    fill_ext(ext, after_ref, north_ref, south_ref, west_ref, east_ref, inside_ref)
    for level in range(levels):
        for row in range(rows):
            total = conv_taps(ext, weights_ref, level, row, columns)
            mixed_ref[level, row] = (ext[level, row + 1, 1 : columns + 1, :] + total).astype(BF16)


def pair_attend(query2, keys2, values2, bias, factor):
    half = query2.shape[0] // 2
    scores = lax.dot_general(query2, keys2, (((1,), (1,)), ((), ())), preferred_element_type=F32)
    if bias is not None:
        scores = scores + bias
    highest = jnp.max(scores, axis=-1, keepdims=True)
    weights = jnp.exp2((scores - highest) * factor)
    summed = jnp.sum(weights, axis=-1, keepdims=True)
    result = jnp.dot(weights.astype(BF16), values2, preferred_element_type=F32)
    low = lax.broadcasted_iota(jnp.int32, (half, LANES), 1) < LANES // 2
    merge = lambda x: jnp.where(low, x[:half], x[half:])
    return merge(highest), merge(summed), merge(result)


def key_bias(flags_ref, slots, sizes):
    if all(slot < 0 for slot in slots):
        return None
    lane = lax.broadcasted_iota(jnp.int32, (1, sum(sizes)), 1)
    bias = jnp.zeros((1, sum(sizes)), F32)
    start = 0
    for slot, size in zip(slots, sizes):
        if slot >= 0:
            value = jnp.where(flags_ref[slot] > 0, 0.0, MASKED).astype(F32)
            bias = jnp.where((lane >= start) & (lane < start + size), value, bias)
        start += size
    return bias


def project(blocks, wk_ref, wv_ref):
    x = blocks[0][...] if len(blocks) == 1 else jnp.concatenate([b[...] for b in blocks], axis=0)
    keys = jnp.dot(x, wk_ref[...], preferred_element_type=F32).astype(BF16)
    values = jnp.dot(x, wv_ref[...], preferred_element_type=F32).astype(BF16)
    return keys, values


def own_kernel(factor, x_ref, wq_ref, wk_ref, wv_ref, query_ref, high_ref, sum_ref, acc_ref):
    tokens = x_ref.shape[0]
    query = jnp.dot(x_ref[...], wq_ref[...], preferred_element_type=F32).astype(BF16)
    keys, values = project([x_ref], wk_ref, wv_ref)
    low = lax.broadcasted_iota(jnp.int32, (tokens, LANES), 1) < LANES // 2
    zero = jnp.zeros((tokens, LANES), BF16)
    for pair in range(GROUP // LANES):
        lanes = slice(pair * LANES, (pair + 1) * LANES)
        part = query[:, lanes]
        query2 = jnp.concatenate([jnp.where(low, part, zero), jnp.where(low, zero, part)], axis=0)
        query_ref[pair] = query2
        high, summed, result = pair_attend(query2, keys[:, lanes], values[:, lanes], None, factor)
        high_ref[:, lanes] = high
        sum_ref[:, lanes] = summed
        acc_ref[:, lanes] = result


def combine(state, part, factor):
    high = jnp.maximum(state[0], part[0])
    old = jnp.exp2((state[0] - high) * factor)
    new = jnp.exp2((part[0] - high) * factor)
    return high, state[1] * old + part[1] * new, state[2] * old + part[2] * new


def batch_kernel(factor, slots, sizes, flags_ref, query_ref, wk_ref, wv_ref, high_in, sum_in, acc_in, *refs):
    blocks, (high_ref, sum_ref, acc_ref) = refs[:-3], refs[-3:]
    keys, values = project(blocks, wk_ref, wv_ref)
    bias = key_bias(flags_ref, slots, sizes)
    for pair in range(GROUP // LANES):
        lanes = slice(pair * LANES, (pair + 1) * LANES)
        part = pair_attend(query_ref[pair], keys[:, lanes], values[:, lanes], bias, factor)
        state = combine((high_in[:, lanes], sum_in[:, lanes], acc_in[:, lanes]), part, factor)
        high_ref[:, lanes], sum_ref[:, lanes], acc_ref[:, lanes] = state


def last_kernel(
    factor, slots, sizes, flags_ref, query_ref, wk_ref, wv_ref, high_in, sum_in, acc_in, wo_ref, stream_ref, *refs
):
    count = len(sizes)
    blocks = refs[:count]
    attended_ref, after_ref, north_ref, south_ref, west_ref, east_ref, total, dense = refs[count:]
    group = pl.program_id(0)
    levels, rows, columns, width = after_ref.shape
    keys, values = project(blocks, wk_ref, wv_ref)
    bias = key_bias(flags_ref, slots, sizes)
    for pair in range(GROUP // LANES):
        lanes = slice(pair * LANES, (pair + 1) * LANES)
        part = pair_attend(query_ref[pair], keys[:, lanes], values[:, lanes], bias, factor)
        _, summed, result = combine((high_in[:, lanes], sum_in[:, lanes], acc_in[:, lanes]), part, factor)
        dense[:, lanes] = result / summed
    for level in range(levels):
        for row in range(rows):
            at = (level * rows + row) * columns
            attended_ref[level, row] = dense[at : at + columns, 0:GROUP].astype(BF16)
    product = jnp.dot(dense[:, 0:GROUP].astype(BF16), wo_ref[...], preferred_element_type=F32)

    @pl.when(group == 0)
    def _():
        total[...] = stream_ref[...].astype(F32) + product

    @pl.when(group > 0)
    def _():
        total[...] += product

    @pl.when(group == pl.num_programs(0) - 1)
    def _():
        for level in range(levels):
            for row in range(rows):
                at = (level * rows + row) * columns
                value = total[at : at + columns, :].astype(BF16)
                after_ref[level, row] = value
                if row == 0:
                    north_ref[level] = value
                if row == rows - 1:
                    south_ref[level] = value
        west = [total[i * columns : i * columns + 1, :] for i in range(levels * rows)]
        east = [total[(i + 1) * columns - 1 : (i + 1) * columns, :] for i in range(levels * rows)]
        west_ref[...] = jnp.concatenate(west, axis=0).astype(BF16)
        east_ref[...] = jnp.concatenate(east, axis=0).astype(BF16)


def shape(dims, kind):
    return jax.ShapeDtypeStruct(dims, kind)


def params():
    return pltpu.CompilerParams(vmem_limit_bytes=VMEM_LIMIT)


def cost(flops, size):
    return pl.CostEstimate(flops=int(flops), bytes_accessed=int(size), transcendentals=0)


def exchange(north_edge, south_edge, west_edge, east_edge, inside):
    levels, columns, width = north_edge.shape
    north = shift(south_edge, "lat", 1)
    south = shift(north_edge, "lat", -1)
    keep_north = inside[0] > 0
    keep_south = inside[1] > 0

    def column(middle, at):
        top = jnp.where(keep_north, north[:, at : at + 1], 0)
        bottom = jnp.where(keep_south, south[:, at : at + 1], 0)
        return jnp.concatenate([top, middle, bottom], axis=1).reshape(-1, width)

    west = shift(column(east_edge, columns - 1), "lon", 1)
    east = shift(column(west_edge, 0), "lon", -1)
    return north, south, west, east


def local(fields, conv_first, w_qkv, w_out, conv_second, key_list, key_count):
    levels, rows, columns, width = fields.shape
    tokens = levels * rows * columns
    groups = width // GROUP
    pairs = GROUP // LANES
    head_size = width // HEADS
    factor = float(np.log2(np.e) * head_size ** -0.5)
    lat_here = lax.axis_index("lat")
    lat_total = lax.axis_size("lat")
    lon_here = lax.axis_index("lon")
    lon_total = lax.axis_size("lon")
    order = ring_order(lon_total)
    place = {lon: i for i, lon in enumerate(order)}
    half = lon_total // 2
    sources = np.zeros((lon_total, lon_total), np.int32)
    for lon in range(lon_total):
        row = [lon]
        for step in range(1, half):
            row += [order[(place[lon] - step) % lon_total], order[(place[lon] + step) % lon_total]]
        row.append(order[(place[lon] + half) % lon_total])
        sources[lon] = row
    inside = jnp.stack([lat_here > 0, lat_here < lat_total - 1]).astype(jnp.int32)
    listed = key_list.reshape(lon_total)
    used = jnp.arange(lon_total, dtype=jnp.int32) < key_count.reshape(())
    mine = jnp.arange(lon_total, dtype=jnp.int32) == lon_here
    source = jnp.sum(jnp.where(mine[:, None], sources, 0), axis=0)
    linked = jnp.any((listed[None, :] == source[:, None]) & used[None, :], axis=1).astype(jnp.int32)
    flags = jnp.concatenate([inside, linked])
    slot_of = lambda position: 2 + position

    smem = spec(pltpu.SMEM)
    vmem = spec(pltpu.VMEM)
    ext = pltpu.VMEM((levels, rows + 2, 16, width), F32)

    north, south, west, east = exchange(
        fields[:, 0], fields[:, rows - 1], fields[:, :, 0], fields[:, :, columns - 1], inside
    )
    stream, normed = pl.pallas_call(
        first_kernel,
        out_shape=(shape((tokens, width), BF16), shape((tokens, width), BF16)),
        in_specs=[smem] + [vmem] * 6,
        out_specs=(vmem, vmem),
        scratch_shapes=[ext, pltpu.VMEM((tokens, width), F32)],
        compiler_params=params(),
        name="conv_first",
    )(inside, fields, north, south, west, east, conv_first)

    whole = lambda n: pl.BlockSpec((n, width), lambda g: (0, 0))
    column = lambda offset: pl.BlockSpec((width, GROUP), lambda g, o=offset: (0, o * groups + g))
    state_spec = pl.BlockSpec((tokens, GROUP), lambda g: (0, g))
    state_shape = shape((tokens, width), F32)
    query_spec = pl.BlockSpec((pairs, 2 * tokens, LANES), lambda g: (g, 0, 0))

    forward = [(order[i], order[(i + 1) % lon_total]) for i in range(lon_total)]
    backward = [(b, a) for a, b in forward]

    query, *state = pl.pallas_call(
        functools.partial(own_kernel, factor),
        grid=(groups,),
        out_shape=(shape((groups * pairs, 2 * tokens, LANES), BF16), *[state_shape] * 3),
        in_specs=[whole(tokens), column(0), column(1), column(2)],
        out_specs=(query_spec, *[state_spec] * 3),
        compiler_params=params(),
        cost_estimate=cost(2 * tokens * width * 3 * width, 6 * width * width),
        name="own_block",
    )(normed, w_qkv, w_qkv, w_qkv)

    def batch(state, blocks, slots):
        sizes = [b.shape[0] for b in blocks]
        return pl.pallas_call(
            functools.partial(batch_kernel, factor, slots, sizes),
            grid=(groups,),
            out_shape=(state_shape,) * 3,
            in_specs=[smem, query_spec, column(1), column(2)] + [state_spec] * 3 + [whole(n) for n in sizes],
            out_specs=(state_spec,) * 3,
            compiler_params=params(),
            cost_estimate=cost(2 * sum(sizes) * width * 2 * width, 4 * width * width),
            name="attend_batch",
        )(flags, query, w_qkv, w_qkv, *state, *blocks)

    ahead, behind = normed, normed
    above = shift(normed, "lat", 1)
    below = shift(normed, "lat", -1)
    waiting = [(above, 0), (below, 1)]
    cut = (tokens // 32) * 16
    for step in range(1, half):
        ahead = lax.ppermute(ahead, "lon", forward)
        behind = lax.ppermute(behind, "lon", backward)
        if step > 1:
            state = batch(state, [b for b, _ in waiting], [s for _, s in waiting])
            waiting = []
        waiting += [(ahead, slot_of(2 * step - 1)), (behind, slot_of(2 * step))]
    far_first = lax.ppermute(ahead[:cut], "lon", forward)
    far_second = lax.ppermute(behind[cut:], "lon", backward)
    state = batch(state, [b for b, _ in waiting], [s for _, s in waiting])
    last_slot = slot_of(lon_total - 1)

    grid4 = (levels, rows, columns, width)
    sizes = [cut, tokens - cut]
    fixed = lambda *dims: pl.BlockSpec(dims, lambda g, n=len(dims): (0,) * n)
    attended, after, north_edge, south_edge, west_edge, east_edge = pl.pallas_call(
        functools.partial(last_kernel, factor, [last_slot] * 2, sizes),
        grid=(groups,),
        out_shape=(
            shape(grid4, BF16),
            shape(grid4, BF16),
            shape((levels, columns, width), BF16),
            shape((levels, columns, width), BF16),
            shape((levels * rows, width), BF16),
            shape((levels * rows, width), BF16),
        ),
        in_specs=[smem, query_spec, column(1), column(2)]
        + [state_spec] * 3
        + [pl.BlockSpec((GROUP, width), lambda g: (g, 0)), whole(tokens)]
        + [whole(n) for n in sizes],
        out_specs=(
            pl.BlockSpec((levels, rows, columns, GROUP), lambda g: (0, 0, 0, g)),
            fixed(*grid4),
            fixed(levels, columns, width),
            fixed(levels, columns, width),
            fixed(levels * rows, width),
            fixed(levels * rows, width),
        ),
        scratch_shapes=[pltpu.VMEM((tokens, width), F32), pltpu.VMEM((tokens, GROUP), F32)],
        compiler_params=params(),
        name="attend_last",
    )(flags, query, w_qkv, w_qkv, *state, w_out, stream, far_first, far_second)

    west_edge = west_edge.reshape(levels, rows, width)
    east_edge = east_edge.reshape(levels, rows, width)
    north, south, west, east = exchange(north_edge, south_edge, west_edge, east_edge, inside)
    mixed = pl.pallas_call(
        second_kernel,
        out_shape=shape(grid4, BF16),
        in_specs=[smem] + [vmem] * 6,
        out_specs=vmem,
        scratch_shapes=[ext],
        compiler_params=params(),
        name="conv_second",
    )(inside, after, north, south, west, east, conv_second)
    return attended, mixed


def solution(mesh):
    return jax.shard_map(
        local,
        mesh=mesh,
        in_specs=(
            P(None, "lat", "lon", None),
            P(),
            P(),
            P(),
            P(),
            P("lat", "lon", None),
            P("lat", "lon"),
        ),
        out_specs=(P(None, "lat", "lon", None), P(None, "lat", "lon", None)),
        check_vma=False,
    )
```

```python
import functools

import jax
import jax.numpy as jnp
import numpy as np
from jax import lax
from jax.experimental import pallas as pl
from jax.experimental.pallas import tpu as pltpu
from jax.sharding import PartitionSpec as P

HEADS = 16
EPSILON = 1e-05
MASKED = -1e30
LANES = 128
SUBLANES = 8
GROUP = 256
F32 = jnp.float32
BF16 = jnp.bfloat16
VMEM_LIMIT = 32 * 1024 * 1024
ABOVE, BELOW = -1, -2


def ring_order(count):
    columns = 1
    while columns * columns * 4 <= count:
        columns *= 2
    rows = count // columns
    order = [z * columns for z in range(rows)]
    for turn, z in enumerate(range(rows - 1, -1, -1)):
        ys = list(range(1, columns))
        if turn % 2:
            ys.reverse()
        order += [z * columns + y for y in ys]
    return order


def shift(x, axis, by):
    size = lax.axis_size(axis)
    return lax.ppermute(x, axis, [(i, (i + by) % size) for i in range(size)])


def fill_ext(ext, center_ref, north_ref, south_ref, pair_ref, across_ref, here_ref):
    levels, columns, rows, width = center_ref.shape
    has_north = (here_ref[0] > 0).astype(F32)
    has_south = (here_ref[1] > 0).astype(F32)
    even = here_ref[2] > 0
    pair = pair_ref[...].astype(F32)
    across = across_ref[...].astype(F32)
    west = jnp.where(even, across, pair)
    east = jnp.where(even, pair, across)
    for level in range(levels):
        north = north_ref[level].astype(F32) * has_north
        south = south_ref[level].astype(F32) * has_south
        for column in range(columns):
            ext[level, column + 1, 0:1, :] = north[column : column + 1]
            ext[level, column + 1, 1 : rows + 1, :] = center_ref[level, column].astype(F32)
            ext[level, column + 1, rows + 1 : rows + 2, :] = south[column : column + 1]
        ext[level, 0, 0 : rows + 2, :] = west[level]
        ext[level, columns + 1, 0 : rows + 2, :] = east[level]


def each_conv(ext, weights_ref, levels, columns, rows, width, emit):
    def tile(index, carry):
        lanes = pl.ds(pl.multiple_of(index * LANES, LANES), LANES)
        taps = [jnp.broadcast_to(weights_ref[k : k + 1, lanes], (SUBLANES, LANES)) for k in range(9)]
        for level in range(levels):
            strip = [ext[level, column, :, lanes] for column in range(columns + 2)]
            for column in range(columns):
                near = strip[column : column + 3]
                sums = [taps[3 * a] * near[0] + taps[3 * a + 1] * near[1] + taps[3 * a + 2] * near[2] for a in range(3)]
                sums[1] = sums[1] + near[1]
                value = sums[0][0:rows] + sums[1][1 : rows + 1] + sums[2][2 : rows + 2]
                emit(level, column, lanes, value)
        return carry

    lax.fori_loop(0, width // LANES, tile, 0)


def first_kernel(here_ref, fields_ref, north_ref, south_ref, pair_ref, across_ref, weights_ref, stream_ref, normed_ref, ext, dense):
    levels, columns, rows, width = fields_ref.shape
    fill_ext(ext, fields_ref, north_ref, south_ref, pair_ref, across_ref, here_ref)

    def emit(level, column, lanes, value):
        at = (level * columns + column) * rows
        dense[at : at + rows, lanes] = value

    each_conv(ext, weights_ref, levels, columns, rows, width, emit)
    stream = dense[...].astype(BF16)
    stream_ref[...] = stream
    wide = stream.astype(F32)
    mean = jnp.mean(wide * wide, axis=-1, keepdims=True)
    normed_ref[...] = (wide * lax.rsqrt(mean + EPSILON)).astype(BF16)


def second_kernel(here_ref, after_ref, north_ref, south_ref, pair_ref, across_ref, weights_ref, mixed_ref, ext):
    levels, columns, rows, width = after_ref.shape
    fill_ext(ext, after_ref, north_ref, south_ref, pair_ref, across_ref, here_ref)

    def emit(level, column, lanes, value):
        mixed_ref[level, column, :, lanes] = value.astype(BF16)

    each_conv(ext, weights_ref, levels, columns, rows, width, emit)


def pair_attend(query2, keys2, values2, bias, factor):
    half = query2.shape[0] // 2
    scores = lax.dot_general(query2, keys2, (((1,), (1,)), ((), ())), preferred_element_type=F32)
    if bias is not None:
        scores = scores + bias
    highest = jnp.max(scores, axis=-1, keepdims=True)
    weights = jnp.exp2((scores - highest) * factor).astype(BF16)
    beside = jnp.concatenate([values2, jnp.ones_like(values2)], axis=1)
    result = jnp.dot(weights, beside, preferred_element_type=F32)
    low = lax.broadcasted_iota(jnp.int32, (half, LANES), 1) < LANES // 2
    merge = lambda x: jnp.where(low, x[:half], x[half:])
    return merge(highest), merge(result[:, LANES:]), merge(result[:, :LANES])


def key_bias(here_ref, sources_ref, list_ref, count_ref, slots, sizes):
    lane = lax.broadcasted_iota(jnp.int32, (1, sum(sizes)), 1)
    bias = jnp.zeros((1, sum(sizes)), F32)
    count = count_ref[0, 0]
    start = 0
    for slot, size in zip(slots, sizes):
        if slot == ABOVE:
            linked = here_ref[0]
        elif slot == BELOW:
            linked = here_ref[1]
        else:
            source = sources_ref[here_ref[3], slot]
            linked = jnp.int32(0)
            for entry in range(list_ref.shape[-1]):
                hit = (list_ref[0, 0, entry] == source) & (entry < count)
                linked = linked | hit.astype(jnp.int32)
        value = jnp.where(linked > 0, 0.0, MASKED).astype(F32)
        bias = jnp.where((lane >= start) & (lane < start + size), value, bias)
        start += size
    return bias


def project(x, w_ref, group):
    width = w_ref.shape[0]
    columns = lambda part: slice(part * width + group * GROUP, part * width + (group + 1) * GROUP)
    keys = jnp.dot(x, w_ref[:, columns(1)], preferred_element_type=F32).astype(BF16)
    values = jnp.dot(x, w_ref[:, columns(2)], preferred_element_type=F32).astype(BF16)
    return keys, values


def joined(blocks):
    return blocks[0][...] if len(blocks) == 1 else jnp.concatenate([b[...] for b in blocks], axis=0)


def head_pairs(width):
    for group in range(width // GROUP):
        for pair in range(GROUP // LANES):
            start = group * GROUP + pair * LANES
            yield group, pair, slice(pair * LANES, (pair + 1) * LANES), slice(start, start + LANES)


def own_kernel(factor, x_ref, w_ref, query_ref, high_ref, sum_ref, acc_ref):
    tokens, width = x_ref.shape
    x = x_ref[...]
    low = lax.broadcasted_iota(jnp.int32, (tokens, LANES), 1) < LANES // 2
    zero = jnp.zeros((tokens, LANES), BF16)
    for group, pair, inner, lanes in head_pairs(width):
        if pair == 0:
            query = jnp.dot(x, w_ref[:, group * GROUP : (group + 1) * GROUP], preferred_element_type=F32).astype(BF16)
            keys, values = project(x, w_ref, group)
        part = query[:, inner]
        query2 = jnp.concatenate([jnp.where(low, part, zero), jnp.where(low, zero, part)], axis=0)
        query_ref[group * (GROUP // LANES) + pair] = query2
        high, summed, result = pair_attend(query2, keys[:, inner], values[:, inner], None, factor)
        high_ref[:, lanes] = high
        sum_ref[:, lanes] = summed
        acc_ref[:, lanes] = result


def combine(state, part, factor):
    high = jnp.maximum(state[0], part[0])
    old = jnp.exp2((state[0] - high) * factor)
    new = jnp.exp2((part[0] - high) * factor)
    return high, state[1] * old + part[1] * new, state[2] * old + part[2] * new


def batch_kernel(
    factor, slots, sizes, here_ref, sources_ref, list_ref, count_ref, query_ref, w_ref, high_in, sum_in, acc_in, *refs
):
    blocks, (high_ref, sum_ref, acc_ref) = refs[:-3], refs[-3:]
    x = joined(blocks)
    bias = key_bias(here_ref, sources_ref, list_ref, count_ref, slots, sizes)
    for group, pair, inner, lanes in head_pairs(x.shape[1]):
        if pair == 0:
            keys, values = project(x, w_ref, group)
        query2 = query_ref[group * (GROUP // LANES) + pair]
        part = pair_attend(query2, keys[:, inner], values[:, inner], bias, factor)
        state = combine((high_in[:, lanes], sum_in[:, lanes], acc_in[:, lanes]), part, factor)
        high_ref[:, lanes], sum_ref[:, lanes], acc_ref[:, lanes] = state


def last_kernel(
    factor, slots, sizes, here_ref, sources_ref, list_ref, count_ref, query_ref, w_ref, high_in, sum_in, acc_in,
    wo_ref, stream_ref, *refs
):
    blocks = refs[: len(sizes)]
    attended_ref, after_ref, north_ref, south_ref, total, dense = refs[len(sizes) :]
    levels, columns, rows, width = after_ref.shape
    x = joined(blocks)
    bias = key_bias(here_ref, sources_ref, list_ref, count_ref, slots, sizes)
    total[...] = stream_ref[...].astype(F32)
    for group, pair, inner, lanes in head_pairs(width):
        if pair == 0:
            keys, values = project(x, w_ref, group)
        query2 = query_ref[group * (GROUP // LANES) + pair]
        part = pair_attend(query2, keys[:, inner], values[:, inner], bias, factor)
        _, summed, result = combine((high_in[:, lanes], sum_in[:, lanes], acc_in[:, lanes]), part, factor)
        dense[:, lanes] = result / summed
        if pair == GROUP // LANES - 1:
            chunk = slice(group * GROUP, (group + 1) * GROUP)
            total[...] += jnp.dot(dense[:, chunk].astype(BF16), wo_ref[chunk, :], preferred_element_type=F32)
    for level in range(levels):
        for column in range(columns):
            at = (level * columns + column) * rows
            attended_ref[level, column] = dense[at : at + rows, :].astype(BF16)
            after_ref[level, column] = total[at : at + rows, :].astype(BF16)
        for edge_ref, row in ((north_ref, 0), (south_ref, rows - 1)):
            places = [(level * columns + column) * rows + row for column in range(columns)]
            picked = jnp.concatenate([total[at : at + 1, :] for at in places], axis=0)
            edge_ref[level] = picked.astype(BF16)


def shape(dims, kind):
    return jax.ShapeDtypeStruct(dims, kind)


def call(kernel, out_shape, scalars, arrays, scratch, name, microseconds):
    return pl.pallas_call(
        kernel,
        out_shape=out_shape,
        in_specs=[pl.BlockSpec(memory_space=pltpu.SMEM)] * len(scalars) + [pl.BlockSpec(memory_space=pltpu.VMEM)] * len(arrays),
        out_specs=jax.tree.map(lambda _: pl.BlockSpec(memory_space=pltpu.VMEM), out_shape),
        scratch_shapes=scratch,
        compiler_params=pltpu.CompilerParams(vmem_limit_bytes=VMEM_LIMIT),
        cost_estimate=pl.CostEstimate(flops=int(microseconds * 1.1e9), bytes_accessed=0, transcendentals=0),
        name=name,
    )(*scalars, *arrays)


def exchange(block, north_edge, south_edge, here):
    columns = block.shape[1]
    count = lax.axis_size("lon")
    north = shift(south_edge, "lat", 1)
    south = shift(north_edge, "lat", -1)

    def column(at):
        top = jnp.where(here[0] > 0, north[:, at : at + 1], 0)
        bottom = jnp.where(here[1] > 0, south[:, at : at + 1], 0)
        return jnp.concatenate([top, block[:, at], bottom], axis=1)

    west, east = column(0), column(columns - 1)
    even = here[2] > 0
    swap = lambda first: [p for i in range(first, count, 2) for p in ((i, (i + 1) % count), ((i + 1) % count, i))]
    pair = lax.ppermute(jnp.where(even, east, west), "lon", swap(0))
    across = lax.ppermute(jnp.where(even, west, east), "lon", swap(1))
    return north, south, pair, across


def local(fields, conv_first, w_qkv, w_out, conv_second, key_list, key_count):
    fields = fields.transpose(0, 2, 1, 3)
    levels, columns, rows, width = fields.shape
    tokens = levels * rows * columns
    pairs = width // LANES
    factor = float(np.log2(np.e) * (width // HEADS) ** -0.5)
    lat_here = lax.axis_index("lat")
    lon_here = lax.axis_index("lon")
    lon_total = lax.axis_size("lon")
    order = ring_order(lon_total)
    place = {lon: i for i, lon in enumerate(order)}
    half = lon_total // 2
    table = np.zeros((lon_total, lon_total), np.int32)
    for lon in range(lon_total):
        for step in range(1, half + 1):
            table[lon, 2 * step - 2] = order[(place[lon] - step) % lon_total]
            table[lon, 2 * step - 1] = order[(place[lon] + step) % lon_total]
    here = jnp.stack(
        [lat_here > 0, lat_here < lax.axis_size("lat") - 1, lon_here % 2 == 0, lon_here]
    ).astype(jnp.int32)
    links = (here, jnp.asarray(table), key_list, key_count)

    ext = pltpu.VMEM((levels, columns + 2, SUBLANES, width), F32)
    dense = pltpu.VMEM((tokens, width), F32)
    halo = exchange(fields, fields[:, :, 0], fields[:, :, rows - 1], here)
    flat = shape((tokens, width), BF16)
    stream, normed = call(first_kernel, (flat, flat), (here,), (fields, *halo, conv_first), [ext, dense], "conv_first", 2)

    forward = [(order[i], order[(i + 1) % lon_total]) for i in range(lon_total)]
    backward = [(b, a) for a, b in forward]
    state_shape = (shape((tokens, width), F32),) * 3
    query, *state = call(
        functools.partial(own_kernel, factor),
        (shape((pairs, 2 * tokens, LANES), BF16), *state_shape),
        (),
        (normed, w_qkv),
        [],
        "own_block",
        4,
    )

    def batch(state, waiting):
        blocks, slots = zip(*waiting)
        sizes = [b.shape[0] for b in blocks]
        return call(
            functools.partial(batch_kernel, factor, slots, sizes),
            state_shape,
            links,
            (query, w_qkv, *state, *blocks),
            [],
            "attend_batch",
            1 + 1.8 * len(blocks),
        )

    ahead, behind = normed, normed
    waiting = [(shift(normed, "lat", 1), ABOVE), (shift(normed, "lat", -1), BELOW)]
    cut = (tokens // 32) * 16
    for step in range(1, half):
        ahead = lax.ppermute(ahead, "lon", forward)
        behind = lax.ppermute(behind, "lon", backward)
        if step > 1:
            state = batch(state, waiting)
            waiting = []
        waiting += [(ahead, 2 * step - 2), (behind, 2 * step - 1)]
    far_first = lax.ppermute(ahead[:cut], "lon", forward)
    far_second = lax.ppermute(behind[cut:], "lon", backward)
    state = batch(state, waiting)

    grid4 = shape(fields.shape, BF16)
    edge = shape((levels, columns, width), BF16)
    attended, after, north_edge, south_edge = call(
        functools.partial(last_kernel, factor, [lon_total - 2] * 2, [cut, tokens - cut]),
        (grid4, grid4, edge, edge),
        links,
        (query, w_qkv, *state, w_out, stream, far_first, far_second),
        [dense, dense],
        "attend_last",
        5,
    )
    halo = exchange(after, north_edge, south_edge, here)
    mixed = call(second_kernel, grid4, (here,), (after, *halo, conv_second), [ext], "conv_second", 2)
    return attended.transpose(0, 2, 1, 3), mixed.transpose(0, 2, 1, 3)


def solution(mesh):
    return jax.shard_map(
        local,
        mesh=mesh,
        in_specs=(
            P(None, "lat", "lon", None),
            P(),
            P(),
            P(),
            P(),
            P("lat", "lon", None),
            P("lat", "lon"),
        ),
        out_specs=(P(None, "lat", "lon", None), P(None, "lat", "lon", None)),
        check_vma=False,
    )
```

```python
import functools

import jax
import jax.numpy as jnp
import numpy as np
from jax import lax
from jax.experimental import pallas as pl
from jax.experimental.pallas import tpu as pltpu
from jax.sharding import PartitionSpec as P

HEADS = 16
EPSILON = 1e-05
MASKED = -1e30
LANES = 128
SUBLANES = 8
GROUP = 256
F32 = jnp.float32
BF16 = jnp.bfloat16
VMEM_LIMIT = 32 * 1024 * 1024
ABOVE, BELOW = -1, -2


def ring_order(count):
    columns = 1
    while columns * columns * 4 <= count:
        columns *= 2
    rows = count // columns
    order = [z * columns for z in range(rows)]
    for turn, z in enumerate(range(rows - 1, -1, -1)):
        ys = list(range(1, columns))
        if turn % 2:
            ys.reverse()
        order += [z * columns + y for y in ys]
    return order


def shift(x, axis, by):
    size = lax.axis_size(axis)
    return lax.ppermute(x, axis, [(i, (i + by) % size) for i in range(size)])


def conv_part(load, dims, weights_ref, part_ref, taps_ref):
    levels, columns, rows = dims
    above = lax.broadcasted_iota(jnp.int32, (SUBLANES, LANES), 0) > 0
    blank = jnp.zeros((SUBLANES - rows, LANES), F32)
    nothing = jnp.zeros((SUBLANES, LANES), F32)

    def tile(index, carry):
        lanes = pl.ds(pl.multiple_of(index * LANES, LANES), LANES)
        taps_ref[index] = weights_ref[:, lanes]
        taps = [jnp.broadcast_to(weights_ref[k : k + 1, lanes], (SUBLANES, LANES)) for k in range(9)]
        for level in range(levels):
            strip = [jnp.concatenate([load(level, column, index, lanes), blank], axis=0) for column in range(columns)]
            strip = [nothing, *strip, nothing]
            for column in range(columns):
                near = strip[column : column + 3]
                sums = [taps[3 * a] * near[0] + taps[3 * a + 1] * near[1] + taps[3 * a + 2] * near[2] for a in range(3)]
                value = near[1] + sums[1]
                value += jnp.where(above, pltpu.roll(sums[0], 1, 0), 0.0)
                value += pltpu.roll(sums[2], SUBLANES - 1, 0)
                at = (level * columns + column) * rows
                part_ref[index, at : at + rows, :] = value[0:rows]
        return carry

    lax.fori_loop(0, part_ref.shape[0], tile, 0)


def first_part_kernel(field_ref, weights_ref, after_ref, part_ref, taps_ref):
    levels, columns, rows, _ = field_ref.shape
    load = lambda level, column, index, lanes: field_ref[level, column, :, lanes].astype(F32)
    conv_part(load, (levels, columns, rows), weights_ref, part_ref, taps_ref)


def weights_kernel(after_ref, far_ref, near_ref, arrived):
    copy = pltpu.make_async_copy(far_ref, near_ref, arrived)
    copy.start()
    copy.wait()


def second_part_kernel(dims, field_ref, weights_ref, dense_ref, part_ref, taps_ref, attended_ref):
    levels, columns, rows = dims

    def load(level, column, index, lanes):
        at = (level * columns + column) * rows
        return field_ref[index, at : at + rows, :]

    conv_part(load, dims, weights_ref, part_ref, taps_ref)
    for level in range(levels):
        for column in range(columns):
            at = (level * columns + column) * rows
            attended_ref[level, column] = dense_ref[at : at + rows, :].astype(BF16)


def add_halo(index, dims, here_ref, north_ref, south_ref, across_ref, pair_ref, part_ref, taps_ref, full):
    levels, columns, rows = dims
    lanes = pl.ds(pl.multiple_of(index * LANES, LANES), LANES)
    even = here_ref[2] > 0
    full[index] = part_ref[index]
    blank = jnp.zeros((1, LANES), F32)
    for level in range(levels):
        start = level * columns * rows
        for ref, flag, a, row in ((north_ref, 0, 0, 0), (south_ref, 1, 2, rows - 1)):
            line = ref[level, :, lanes].astype(F32)
            left = jnp.concatenate([blank, line[:-1]], axis=0)
            right = jnp.concatenate([line[1:], blank], axis=0)
            tap = [taps_ref[index, 3 * a + b : 3 * a + b + 1, :] for b in range(3)]
            more = tap[0] * left + tap[1] * line + tap[2] * right
            more = jnp.where(here_ref[flag] > 0, more, 0.0)
            full[index, pl.ds(start + row, columns, stride=rows), :] += more
        pair = pair_ref[level, :, lanes].astype(F32)
        across = across_ref[level, :, lanes].astype(F32)
        west = jnp.where(even, across, pair)
        east = jnp.where(even, pair, across)
        for side, b, column in ((west, 0, 0), (east, 2, columns - 1)):
            more = None
            for a in range(3):
                term = taps_ref[index, 3 * a + b : 3 * a + b + 1, :] * side[a : a + rows]
                more = term if more is None else more + term
            full[index, start + column * rows : start + (column + 1) * rows, :] += more


def first_kernel(dims, here_ref, part_ref, taps_ref, north_ref, south_ref, across_ref, pair_ref, stream_ref, normed_ref, full):
    tiles, tokens, _ = part_ref.shape
    squares = jnp.zeros((tokens, LANES), F32)
    for index in range(tiles):
        lanes = slice(index * LANES, (index + 1) * LANES)
        add_halo(index, dims, here_ref, north_ref, south_ref, across_ref, pair_ref, part_ref, taps_ref, full)
        stream = full[index].astype(BF16)
        stream_ref[:, lanes] = stream
        wide = stream.astype(F32)
        squares += wide * wide
    mean = jnp.sum(squares, axis=-1, keepdims=True) * (1.0 / (tiles * LANES))
    scale = jnp.broadcast_to(lax.rsqrt(mean + EPSILON), (tokens, LANES))
    for index in range(tiles):
        lanes = slice(index * LANES, (index + 1) * LANES)
        normed_ref[:, lanes] = (stream_ref[:, lanes].astype(F32) * scale).astype(BF16)


def second_kernel(dims, here_ref, part_ref, taps_ref, north_ref, south_ref, across_ref, pair_ref, mixed_ref, full):
    levels, columns, rows = dims
    for index in range(part_ref.shape[0]):
        lanes = slice(index * LANES, (index + 1) * LANES)
        add_halo(index, dims, here_ref, north_ref, south_ref, across_ref, pair_ref, part_ref, taps_ref, full)
        for level in range(levels):
            for column in range(columns):
                at = (level * columns + column) * rows
                mixed_ref[level, column, :, lanes] = full[index, at : at + rows, :].astype(BF16)


def pair_attend(query2, keys2, values2, bias, factor):
    half = query2.shape[0] // 2
    scores = lax.dot_general(query2, keys2, (((1,), (1,)), ((), ())), preferred_element_type=F32)
    if bias is not None:
        scores = scores + bias
    highest = jnp.max(scores, axis=-1, keepdims=True)
    weights = jnp.exp2((scores - highest) * factor).astype(BF16)
    beside = jnp.concatenate([values2, jnp.ones_like(values2)], axis=1)
    result = jnp.dot(weights, beside, preferred_element_type=F32)
    low = lax.broadcasted_iota(jnp.int32, (half, LANES), 1) < LANES // 2
    merge = lambda x: jnp.where(low, x[:half], x[half:])
    return merge(highest), merge(result[:, LANES:]), merge(result[:, :LANES])


def key_bias(here_ref, sources_ref, list_ref, count_ref, slots, sizes):
    lane = lax.broadcasted_iota(jnp.int32, (1, sum(sizes)), 1)
    bias = jnp.zeros((1, sum(sizes)), F32)
    count = count_ref[0, 0]
    start = 0
    for slot, size in zip(slots, sizes):
        if slot == ABOVE:
            linked = here_ref[0]
        elif slot == BELOW:
            linked = here_ref[1]
        else:
            source = sources_ref[here_ref[3], slot]
            linked = jnp.int32(0)
            for entry in range(list_ref.shape[-1]):
                hit = (list_ref[0, 0, entry] == source) & (entry < count)
                linked = linked | hit.astype(jnp.int32)
        value = jnp.where(linked > 0, 0.0, MASKED).astype(F32)
        bias = jnp.where((lane >= start) & (lane < start + size), value, bias)
        start += size
    return bias


def project(x, w_ref, group):
    width = w_ref.shape[0]
    columns = lambda part: slice(part * width + group * GROUP, part * width + (group + 1) * GROUP)
    keys = jnp.dot(x, w_ref[:, columns(1)], preferred_element_type=F32).astype(BF16)
    values = jnp.dot(x, w_ref[:, columns(2)], preferred_element_type=F32).astype(BF16)
    return keys, values


def joined(blocks):
    return blocks[0][...] if len(blocks) == 1 else jnp.concatenate([b[...] for b in blocks], axis=0)


def head_pairs(width):
    for group in range(width // GROUP):
        for pair in range(GROUP // LANES):
            start = group * GROUP + pair * LANES
            yield group, pair, slice(pair * LANES, (pair + 1) * LANES), slice(start, start + LANES)


def own_kernel(factor, x_ref, w_ref, handed_ref, query_ref, high_ref, sum_ref, acc_ref):
    tokens, width = x_ref.shape
    x = x_ref[...]
    handed_ref[...] = x
    low = lax.broadcasted_iota(jnp.int32, (tokens, LANES), 1) < LANES // 2
    zero = jnp.zeros((tokens, LANES), BF16)
    for group, pair, inner, lanes in head_pairs(width):
        if pair == 0:
            query = jnp.dot(x, w_ref[:, group * GROUP : (group + 1) * GROUP], preferred_element_type=F32).astype(BF16)
            keys, values = project(x, w_ref, group)
        part = query[:, inner]
        query2 = jnp.concatenate([jnp.where(low, part, zero), jnp.where(low, zero, part)], axis=0)
        query_ref[group * (GROUP // LANES) + pair] = query2
        high, summed, result = pair_attend(query2, keys[:, inner], values[:, inner], None, factor)
        high_ref[:, lanes] = high
        sum_ref[:, lanes] = summed
        acc_ref[:, lanes] = result


def combine(state, part, factor):
    high = jnp.maximum(state[0], part[0])
    old = jnp.exp2((state[0] - high) * factor)
    new = jnp.exp2((part[0] - high) * factor)
    return high, state[1] * old + part[1] * new, state[2] * old + part[2] * new


def batch_kernel(
    factor, slots, sizes, here_ref, sources_ref, list_ref, count_ref, query_ref, w_ref, high_in, sum_in, acc_in, *refs
):
    blocks, (high_ref, sum_ref, acc_ref) = refs[:-3], refs[-3:]
    x = joined(blocks)
    bias = key_bias(here_ref, sources_ref, list_ref, count_ref, slots, sizes)
    for group, pair, inner, lanes in head_pairs(x.shape[1]):
        if pair == 0:
            keys, values = project(x, w_ref, group)
        query2 = query_ref[group * (GROUP // LANES) + pair]
        part = pair_attend(query2, keys[:, inner], values[:, inner], bias, factor)
        state = combine((high_in[:, lanes], sum_in[:, lanes], acc_in[:, lanes]), part, factor)
        high_ref[:, lanes], sum_ref[:, lanes], acc_ref[:, lanes] = state


def last_kernel(
    factor, dims, slots, sizes, here_ref, sources_ref, list_ref, count_ref, query_ref, w_ref, high_in, sum_in, acc_in,
    wo_ref, stream_ref, *refs
):
    blocks = refs[: len(sizes)]
    dense, after_ref, north_ref, south_ref, west_ref, east_ref, total = refs[len(sizes) :]
    levels, columns, rows = dims
    x = joined(blocks)
    width = x.shape[1]
    bias = key_bias(here_ref, sources_ref, list_ref, count_ref, slots, sizes)
    total[...] = stream_ref[...].astype(F32)
    for group, pair, inner, lanes in head_pairs(width):
        if pair == 0:
            keys, values = project(x, w_ref, group)
        query2 = query_ref[group * (GROUP // LANES) + pair]
        part = pair_attend(query2, keys[:, inner], values[:, inner], bias, factor)
        _, summed, result = combine((high_in[:, lanes], sum_in[:, lanes], acc_in[:, lanes]), part, factor)
        dense[:, lanes] = result / summed
        if pair == GROUP // LANES - 1:
            chunk = slice(group * GROUP, (group + 1) * GROUP)
            total[...] += jnp.dot(dense[:, chunk].astype(BF16), wo_ref[chunk, :], preferred_element_type=F32)
    for index in range(width // LANES):
        lanes = slice(index * LANES, (index + 1) * LANES)
        after_ref[index] = total[:, lanes].astype(BF16).astype(F32)
        for level in range(levels):
            start = level * columns * rows
            stop = start + columns * rows
            north_ref[level, :, lanes] = after_ref[index, pl.ds(start, columns, stride=rows), :].astype(BF16)
            south_ref[level, :, lanes] = after_ref[index, pl.ds(start + rows - 1, columns, stride=rows), :].astype(BF16)
            west_ref[level, :, lanes] = after_ref[index, start : start + rows, :].astype(BF16)
            east_ref[level, :, lanes] = after_ref[index, stop - rows : stop, :].astype(BF16)


def shape(dims, kind):
    return jax.ShapeDtypeStruct(dims, kind)


def call(kernel, out_shape, scalars, arrays, scratch, name, microseconds):
    return pl.pallas_call(
        kernel,
        out_shape=out_shape,
        in_specs=[pl.BlockSpec(memory_space=pltpu.SMEM)] * len(scalars) + [pl.BlockSpec(memory_space=pltpu.VMEM)] * len(arrays),
        out_specs=jax.tree.map(lambda _: pl.BlockSpec(memory_space=pltpu.VMEM), out_shape),
        scratch_shapes=scratch,
        compiler_params=pltpu.CompilerParams(vmem_limit_bytes=VMEM_LIMIT),
        cost_estimate=pl.CostEstimate(flops=int(microseconds * 1.1e9), bytes_accessed=0, transcendentals=0),
        name=name,
    )(*scalars, *arrays)


def exchange(north_edge, south_edge, west_edge, east_edge, here):
    columns = north_edge.shape[1]
    count = lax.axis_size("lon")
    north = shift(south_edge, "lat", 1)
    south = shift(north_edge, "lat", -1)

    def column(edge, at):
        top = jnp.where(here[0] > 0, north[:, at : at + 1], 0)
        bottom = jnp.where(here[1] > 0, south[:, at : at + 1], 0)
        return jnp.concatenate([top, edge, bottom], axis=1)

    west, east = column(west_edge, 0), column(east_edge, columns - 1)
    even = here[2] > 0
    swap = lambda first: [p for i in range(first, count, 2) for p in ((i, (i + 1) % count), ((i + 1) % count, i))]
    across = lax.ppermute(jnp.where(even, west, east), "lon", swap(1))
    pair = lax.ppermute(jnp.where(even, east, west), "lon", swap(0))
    return north, south, across, pair


def local(fields, conv_first, w_qkv, w_out, conv_second, key_list, key_count):
    fields = fields.transpose(0, 2, 1, 3)
    levels, columns, rows, width = fields.shape
    tokens = levels * rows * columns
    pairs = width // LANES
    factor = float(np.log2(np.e) * (width // HEADS) ** -0.5)
    lat_here = lax.axis_index("lat")
    lon_here = lax.axis_index("lon")
    lon_total = lax.axis_size("lon")
    order = ring_order(lon_total)
    place = {lon: i for i, lon in enumerate(order)}
    half = lon_total // 2
    table = np.zeros((lon_total, lon_total), np.int32)
    for lon in range(lon_total):
        for step in range(1, half + 1):
            table[lon, 2 * step - 2] = order[(place[lon] - step) % lon_total]
            table[lon, 2 * step - 1] = order[(place[lon] + step) % lon_total]
    here = jnp.stack(
        [lat_here > 0, lat_here < lax.axis_size("lat") - 1, lon_here % 2 == 0, lon_here]
    ).astype(jnp.int32)
    links = (here, jnp.asarray(table), key_list, key_count)

    dims = (levels, columns, rows)
    tiles = width // LANES
    full = pltpu.VMEM((tiles, tokens, LANES), F32)
    part_shape = (shape((tiles, tokens, LANES), F32), shape((tiles, 9, LANES), F32))
    halo = exchange(fields[:, :, 0], fields[:, :, rows - 1], fields[:, 0], fields[:, columns - 1], here)
    vmem = pl.BlockSpec(memory_space=pltpu.VMEM)
    anywhere = pl.BlockSpec(memory_space=pl.ANY)
    part = pl.pallas_call(
        first_part_kernel,
        out_shape=part_shape,
        in_specs=[vmem, vmem, anywhere],
        out_specs=(vmem,) * 2,
        compiler_params=pltpu.CompilerParams(vmem_limit_bytes=VMEM_LIMIT),
        cost_estimate=pl.CostEstimate(flops=int(2e9), bytes_accessed=0, transcendentals=0),
        name="conv_part",
    )(fields, conv_first, halo[0])
    w_qkv = pl.pallas_call(
        weights_kernel,
        out_shape=shape(w_qkv.shape, BF16),
        in_specs=[anywhere, anywhere],
        out_specs=vmem,
        scratch_shapes=[pltpu.SemaphoreType.DMA],
        compiler_params=pltpu.CompilerParams(vmem_limit_bytes=VMEM_LIMIT),
        cost_estimate=pl.CostEstimate(flops=int(2e9), bytes_accessed=0, transcendentals=0),
        name="weights_near",
    )(halo[0], w_qkv)
    flat = shape((tokens, width), BF16)
    stream, normed = call(
        functools.partial(first_kernel, dims), (flat, flat), (here,), (*part, *halo), [full], "conv_first", 2
    )

    forward = [(order[i], order[(i + 1) % lon_total]) for i in range(lon_total)]
    backward = [(b, a) for a, b in forward]
    state_shape = (shape((tokens, width), F32),) * 3
    handed, query, *state = call(
        functools.partial(own_kernel, factor),
        (flat, shape((pairs, 2 * tokens, LANES), BF16), *state_shape),
        (),
        (normed, w_qkv),
        [],
        "own_block",
        4,
    )

    def batch(state, waiting):
        blocks, slots = zip(*waiting)
        sizes = [b.shape[0] for b in blocks]
        return call(
            functools.partial(batch_kernel, factor, slots, sizes),
            state_shape,
            links,
            (query, w_qkv, *state, *blocks),
            [],
            "attend_batch",
            1 + 1.8 * len(blocks),
        )

    ahead, behind = normed, normed
    waiting = []
    cut = (tokens // 32) * 16
    for step in range(1, half):
        ahead = lax.ppermute(ahead, "lon", forward)
        behind = lax.ppermute(behind, "lon", backward)
        if step > 1:
            state = batch(state, waiting)
        waiting = [(ahead, 2 * step - 2), (behind, 2 * step - 1)]
        if step == 2:
            waiting += [(shift(handed, "lat", 1), ABOVE), (shift(handed, "lat", -1), BELOW)]
    far_first = lax.ppermute(ahead[:cut], "lon", forward)
    far_second = lax.ppermute(behind[cut:], "lon", backward)
    state = batch(state, waiting)

    row_edge, column_edge = shape((levels, columns, width), BF16), shape((levels, rows, width), BF16)
    dense, after, *edges = call(
        functools.partial(last_kernel, factor, dims, [lon_total - 2] * 2, [cut, tokens - cut]),
        (shape((tokens, width), F32), part_shape[0], row_edge, row_edge, column_edge, column_edge),
        links,
        (query, w_qkv, *state, w_out, stream, far_first, far_second),
        [pltpu.VMEM((tokens, width), F32)],
        "attend_last",
        5,
    )
    halo = exchange(*edges, here)
    grid4 = shape(fields.shape, BF16)
    *part, attended = call(
        functools.partial(second_part_kernel, dims),
        (*part_shape, grid4),
        (),
        (after, conv_second, dense),
        [],
        "conv_part",
        2,
    )
    mixed = call(functools.partial(second_kernel, dims), grid4, (here,), (*part, *halo), [full], "conv_second", 2)
    return attended.transpose(0, 2, 1, 3), mixed.transpose(0, 2, 1, 3)


def solution(mesh):
    return jax.shard_map(
        local,
        mesh=mesh,
        in_specs=(
            P(None, "lat", "lon", None),
            P(),
            P(),
            P(),
            P(),
            P("lat", "lon", None),
            P("lat", "lon"),
        ),
        out_specs=(P(None, "lat", "lon", None), P(None, "lat", "lon", None)),
        check_vma=False,
    )
```

```python
import functools

import jax
import jax.numpy as jnp
import numpy as np
from jax import lax
from jax.experimental import pallas as pl
from jax.experimental.pallas import tpu as pltpu
from jax.sharding import PartitionSpec as P

HEADS = 16
EPSILON = 1e-05
MASKED = -1e30
LANES = 128
SUBLANES = 8
GROUP = 256
F32 = jnp.float32
BF16 = jnp.bfloat16
VMEM_LIMIT = 32 * 1024 * 1024
ABOVE, BELOW = -1, -2


def ring_order(count):
    columns = 1
    while columns * columns * 4 <= count:
        columns *= 2
    rows = count // columns
    order = [z * columns for z in range(rows)]
    for turn, z in enumerate(range(rows - 1, -1, -1)):
        ys = list(range(1, columns))
        if turn % 2:
            ys.reverse()
        order += [z * columns + y for y in ys]
    return order


def shift(x, axis, by):
    size = lax.axis_size(axis)
    return lax.ppermute(x, axis, [(i, (i + by) % size) for i in range(size)])


def conv_part(load, dims, weights_ref, part_ref, taps_ref):
    levels, columns, rows = dims
    above = lax.broadcasted_iota(jnp.int32, (SUBLANES, LANES), 0) > 0
    blank = jnp.zeros((SUBLANES - rows, LANES), F32)
    nothing = jnp.zeros((SUBLANES, LANES), F32)

    def tile(index, carry):
        lanes = pl.ds(pl.multiple_of(index * LANES, LANES), LANES)
        taps_ref[index] = weights_ref[:, lanes]
        taps = [jnp.broadcast_to(weights_ref[k : k + 1, lanes], (SUBLANES, LANES)) for k in range(9)]
        for level in range(levels):
            strip = [jnp.concatenate([load(level, column, index, lanes), blank], axis=0) for column in range(columns)]
            strip = [nothing, *strip, nothing]
            for column in range(columns):
                near = strip[column : column + 3]
                sums = [taps[3 * a] * near[0] + taps[3 * a + 1] * near[1] + taps[3 * a + 2] * near[2] for a in range(3)]
                value = near[1] + sums[1]
                value += jnp.where(above, pltpu.roll(sums[0], 1, 0), 0.0)
                value += pltpu.roll(sums[2], SUBLANES - 1, 0)
                at = (level * columns + column) * rows
                part_ref[index, at : at + rows, :] = value[0:rows]
        return carry

    lax.fori_loop(0, part_ref.shape[0], tile, 0)


def first_part_kernel(field_ref, weights_ref, after_ref, part_ref, taps_ref):
    levels, columns, rows, _ = field_ref.shape
    load = lambda level, column, index, lanes: field_ref[level, column, :, lanes].astype(F32)
    conv_part(load, (levels, columns, rows), weights_ref, part_ref, taps_ref)


def weights_kernel(after_ref, far_ref, near_ref, arrived):
    copy = pltpu.make_async_copy(far_ref, near_ref, arrived)
    copy.start()
    copy.wait()


def second_part_kernel(dims, field_ref, weights_ref, dense_ref, part_ref, taps_ref, attended_ref):
    levels, columns, rows = dims

    def load(level, column, index, lanes):
        at = (level * columns + column) * rows
        return field_ref[index, at : at + rows, :]

    conv_part(load, dims, weights_ref, part_ref, taps_ref)
    for level in range(levels):
        for column in range(columns):
            at = (level * columns + column) * rows
            attended_ref[level, column] = dense_ref[at : at + rows, :].astype(BF16)


def add_halo(index, dims, here_ref, north_ref, south_ref, across_ref, pair_ref, part_ref, taps_ref, full):
    levels, columns, rows = dims
    lanes = pl.ds(pl.multiple_of(index * LANES, LANES), LANES)
    even = here_ref[2] > 0
    full[index] = part_ref[index]
    blank = jnp.zeros((1, LANES), F32)
    for level in range(levels):
        start = level * columns * rows
        for ref, flag, a, row in ((north_ref, 0, 0, 0), (south_ref, 1, 2, rows - 1)):
            line = ref[level, :, lanes].astype(F32)
            left = jnp.concatenate([blank, line[:-1]], axis=0)
            right = jnp.concatenate([line[1:], blank], axis=0)
            tap = [taps_ref[index, 3 * a + b : 3 * a + b + 1, :] for b in range(3)]
            more = tap[0] * left + tap[1] * line + tap[2] * right
            more = jnp.where(here_ref[flag] > 0, more, 0.0)
            full[index, pl.ds(start + row, columns, stride=rows), :] += more
        pair = pair_ref[level, :, lanes].astype(F32)
        across = across_ref[level, :, lanes].astype(F32)
        west = jnp.where(even, across, pair)
        east = jnp.where(even, pair, across)
        for side, b, column in ((west, 0, 0), (east, 2, columns - 1)):
            more = None
            for a in range(3):
                term = taps_ref[index, 3 * a + b : 3 * a + b + 1, :] * side[a : a + rows]
                more = term if more is None else more + term
            full[index, start + column * rows : start + (column + 1) * rows, :] += more


def first_kernel(dims, here_ref, part_ref, taps_ref, north_ref, south_ref, across_ref, pair_ref, stream_ref, normed_ref, full):
    tiles, tokens, _ = part_ref.shape
    squares = jnp.zeros((tokens, LANES), F32)
    for index in range(tiles):
        lanes = slice(index * LANES, (index + 1) * LANES)
        add_halo(index, dims, here_ref, north_ref, south_ref, across_ref, pair_ref, part_ref, taps_ref, full)
        stream = full[index].astype(BF16)
        stream_ref[:, lanes] = stream
        wide = stream.astype(F32)
        squares += wide * wide
    mean = jnp.sum(squares, axis=-1, keepdims=True) * (1.0 / (tiles * LANES))
    scale = jnp.broadcast_to(lax.rsqrt(mean + EPSILON), (tokens, LANES))
    for index in range(tiles):
        lanes = slice(index * LANES, (index + 1) * LANES)
        normed_ref[:, lanes] = (stream_ref[:, lanes].astype(F32) * scale).astype(BF16)


def second_kernel(dims, here_ref, part_ref, taps_ref, north_ref, south_ref, across_ref, pair_ref, mixed_ref, full):
    levels, columns, rows = dims
    for index in range(part_ref.shape[0]):
        lanes = slice(index * LANES, (index + 1) * LANES)
        add_halo(index, dims, here_ref, north_ref, south_ref, across_ref, pair_ref, part_ref, taps_ref, full)
        for level in range(levels):
            for column in range(columns):
                at = (level * columns + column) * rows
                mixed_ref[level, column, :, lanes] = full[index, at : at + rows, :].astype(BF16)


def scores_of(query2, keys2, bias):
    scores = lax.dot_general(query2, keys2, (((1,), (1,)), ((), ())), preferred_element_type=F32)
    return scores if bias is None else scores + bias


def merge(both):
    half = both.shape[0] // 2
    low = lax.broadcasted_iota(jnp.int32, (half, LANES), 1) < LANES // 2
    return jnp.where(low, both[:half], both[half:])


def attend_pairs(factor, x, w_ref, bias, query_of, finish):
    width = x.shape[1]
    pairs = width // LANES
    inside = GROUP // LANES
    groups, scores = {}, {}

    def project(group):
        if group * GROUP < width and group not in groups:
            columns = lambda part: slice(part * width + group * GROUP, part * width + (group + 1) * GROUP)
            groups[group] = [
                jnp.dot(x, w_ref[:, columns(part)], preferred_element_type=F32).astype(BF16) for part in (1, 2)
            ]

    def lanes_of(pair):
        return slice(pair % inside * LANES, (pair % inside + 1) * LANES)

    def score(pair):
        if pair < pairs:
            project(pair // inside)
            scores[pair] = scores_of(query_of(pair), groups[pair // inside][0][:, lanes_of(pair)], bias)

    def weigh(pair, highest, weights):
        values2 = groups[pair // inside][1][:, lanes_of(pair)]
        beside = jnp.concatenate([values2, jnp.ones_like(values2)], axis=1)
        result = jnp.dot(weights, beside, preferred_element_type=F32)
        finish(pair, (merge(highest), merge(result[:, LANES:]), merge(result[:, :LANES])))

    score(0)
    waiting = None
    for pair in range(pairs):
        if (pair + 1) % inside == 1:
            project((pair + 1) // inside + 1)
        score(pair + 1)
        current = scores.pop(pair)
        highest = jnp.max(current, axis=-1, keepdims=True)
        weights = jnp.exp2((current - highest) * factor).astype(BF16)
        if waiting is not None:
            weigh(*waiting)
        waiting = (pair, highest, weights)
    weigh(*waiting)


def key_bias(here_ref, sources_ref, list_ref, count_ref, slots, sizes):
    lane = lax.broadcasted_iota(jnp.int32, (1, sum(sizes)), 1)
    bias = jnp.zeros((1, sum(sizes)), F32)
    count = count_ref[0, 0]
    start = 0
    for slot, size in zip(slots, sizes):
        if slot == ABOVE:
            linked = here_ref[0]
        elif slot == BELOW:
            linked = here_ref[1]
        else:
            source = sources_ref[here_ref[3], slot]
            linked = jnp.int32(0)
            for entry in range(list_ref.shape[-1]):
                hit = (list_ref[0, 0, entry] == source) & (entry < count)
                linked = linked | hit.astype(jnp.int32)
        value = jnp.where(linked > 0, 0.0, MASKED).astype(F32)
        bias = jnp.where((lane >= start) & (lane < start + size), value, bias)
        start += size
    return bias


def joined(blocks):
    return blocks[0][...] if len(blocks) == 1 else jnp.concatenate([b[...] for b in blocks], axis=0)


def own_kernel(factor, x_ref, w_ref, handed_ref, query_ref, high_ref, sum_ref, acc_ref):
    tokens, width = x_ref.shape
    x = x_ref[...]
    handed_ref[...] = x
    low = lax.broadcasted_iota(jnp.int32, (tokens, LANES), 1) < LANES // 2
    zero = jnp.zeros((tokens, LANES), BF16)
    inside = GROUP // LANES
    queries = {}

    def query_of(pair):
        group = pair // inside
        if group not in queries:
            columns = slice(group * GROUP, (group + 1) * GROUP)
            queries[group] = jnp.dot(x, w_ref[:, columns], preferred_element_type=F32).astype(BF16)
        part = queries[group][:, pair % inside * LANES : (pair % inside + 1) * LANES]
        query2 = jnp.concatenate([jnp.where(low, part, zero), jnp.where(low, zero, part)], axis=0)
        query_ref[pair] = query2
        return query2

    def finish(pair, part):
        lanes = slice(pair * LANES, (pair + 1) * LANES)
        high_ref[:, lanes], sum_ref[:, lanes], acc_ref[:, lanes] = part

    attend_pairs(factor, x, w_ref, None, query_of, finish)


def combine(state, part, factor):
    high = jnp.maximum(state[0], part[0])
    old = jnp.exp2((state[0] - high) * factor)
    new = jnp.exp2((part[0] - high) * factor)
    return high, state[1] * old + part[1] * new, state[2] * old + part[2] * new


def batch_kernel(
    factor, slots, sizes, here_ref, sources_ref, list_ref, count_ref, query_ref, w_ref, high_in, sum_in, acc_in, *refs
):
    blocks, (high_ref, sum_ref, acc_ref) = refs[:-3], refs[-3:]
    bias = key_bias(here_ref, sources_ref, list_ref, count_ref, slots, sizes)

    def finish(pair, part):
        lanes = slice(pair * LANES, (pair + 1) * LANES)
        state = combine((high_in[:, lanes], sum_in[:, lanes], acc_in[:, lanes]), part, factor)
        high_ref[:, lanes], sum_ref[:, lanes], acc_ref[:, lanes] = state

    attend_pairs(factor, joined(blocks), w_ref, bias, lambda pair: query_ref[pair], finish)


def last_kernel(
    factor, dims, slots, sizes, here_ref, sources_ref, list_ref, count_ref, query_ref, w_ref, high_in, sum_in, acc_in,
    wo_ref, stream_ref, *refs
):
    blocks = refs[: len(sizes)]
    dense, after_ref, north_ref, south_ref, west_ref, east_ref, total = refs[len(sizes) :]
    levels, columns, rows = dims
    x = joined(blocks)
    width = x.shape[1]
    bias = key_bias(here_ref, sources_ref, list_ref, count_ref, slots, sizes)
    total[...] = stream_ref[...].astype(F32)

    def finish(pair, part):
        lanes = slice(pair * LANES, (pair + 1) * LANES)
        _, summed, result = combine((high_in[:, lanes], sum_in[:, lanes], acc_in[:, lanes]), part, factor)
        dense[:, lanes] = result / summed
        if (pair + 1) * LANES % GROUP == 0:
            chunk = slice((pair + 1) * LANES - GROUP, (pair + 1) * LANES)
            total[...] += jnp.dot(dense[:, chunk].astype(BF16), wo_ref[chunk, :], preferred_element_type=F32)

    attend_pairs(factor, x, w_ref, bias, lambda pair: query_ref[pair], finish)
    for index in range(width // LANES):
        lanes = slice(index * LANES, (index + 1) * LANES)
        after_ref[index] = total[:, lanes].astype(BF16).astype(F32)
        for level in range(levels):
            start = level * columns * rows
            stop = start + columns * rows
            north_ref[level, :, lanes] = after_ref[index, pl.ds(start, columns, stride=rows), :].astype(BF16)
            south_ref[level, :, lanes] = after_ref[index, pl.ds(start + rows - 1, columns, stride=rows), :].astype(BF16)
            west_ref[level, :, lanes] = after_ref[index, start : start + rows, :].astype(BF16)
            east_ref[level, :, lanes] = after_ref[index, stop - rows : stop, :].astype(BF16)


def shape(dims, kind):
    return jax.ShapeDtypeStruct(dims, kind)


def call(kernel, out_shape, scalars, arrays, scratch, name, microseconds):
    return pl.pallas_call(
        kernel,
        out_shape=out_shape,
        in_specs=[pl.BlockSpec(memory_space=pltpu.SMEM)] * len(scalars) + [pl.BlockSpec(memory_space=pltpu.VMEM)] * len(arrays),
        out_specs=jax.tree.map(lambda _: pl.BlockSpec(memory_space=pltpu.VMEM), out_shape),
        scratch_shapes=scratch,
        compiler_params=pltpu.CompilerParams(vmem_limit_bytes=VMEM_LIMIT),
        cost_estimate=pl.CostEstimate(flops=int(microseconds * 1.1e9), bytes_accessed=0, transcendentals=0),
        name=name,
    )(*scalars, *arrays)


def exchange(north_edge, south_edge, west_edge, east_edge, here):
    columns = north_edge.shape[1]
    count = lax.axis_size("lon")
    north = shift(south_edge, "lat", 1)
    south = shift(north_edge, "lat", -1)

    def column(edge, at):
        top = jnp.where(here[0] > 0, north[:, at : at + 1], 0)
        bottom = jnp.where(here[1] > 0, south[:, at : at + 1], 0)
        return jnp.concatenate([top, edge, bottom], axis=1)

    west, east = column(west_edge, 0), column(east_edge, columns - 1)
    even = here[2] > 0
    swap = lambda first: [p for i in range(first, count, 2) for p in ((i, (i + 1) % count), ((i + 1) % count, i))]
    across = lax.ppermute(jnp.where(even, west, east), "lon", swap(1))
    pair = lax.ppermute(jnp.where(even, east, west), "lon", swap(0))
    return north, south, across, pair


def local(fields, conv_first, w_qkv, w_out, conv_second, key_list, key_count):
    fields = fields.transpose(0, 2, 1, 3)
    levels, columns, rows, width = fields.shape
    tokens = levels * rows * columns
    pairs = width // LANES
    factor = float(np.log2(np.e) * (width // HEADS) ** -0.5)
    lat_here = lax.axis_index("lat")
    lon_here = lax.axis_index("lon")
    lon_total = lax.axis_size("lon")
    order = ring_order(lon_total)
    place = {lon: i for i, lon in enumerate(order)}
    half = lon_total // 2
    table = np.zeros((lon_total, lon_total), np.int32)
    for lon in range(lon_total):
        for step in range(1, half + 1):
            table[lon, 2 * step - 2] = order[(place[lon] - step) % lon_total]
            table[lon, 2 * step - 1] = order[(place[lon] + step) % lon_total]
    here = jnp.stack(
        [lat_here > 0, lat_here < lax.axis_size("lat") - 1, lon_here % 2 == 0, lon_here]
    ).astype(jnp.int32)
    links = (here, jnp.asarray(table), key_list, key_count)

    dims = (levels, columns, rows)
    tiles = width // LANES
    full = pltpu.VMEM((tiles, tokens, LANES), F32)
    part_shape = (shape((tiles, tokens, LANES), F32), shape((tiles, 9, LANES), F32))
    halo = exchange(fields[:, :, 0], fields[:, :, rows - 1], fields[:, 0], fields[:, columns - 1], here)
    vmem = pl.BlockSpec(memory_space=pltpu.VMEM)
    anywhere = pl.BlockSpec(memory_space=pl.ANY)
    part = pl.pallas_call(
        first_part_kernel,
        out_shape=part_shape,
        in_specs=[vmem, vmem, anywhere],
        out_specs=(vmem,) * 2,
        compiler_params=pltpu.CompilerParams(vmem_limit_bytes=VMEM_LIMIT),
        cost_estimate=pl.CostEstimate(flops=int(2e9), bytes_accessed=0, transcendentals=0),
        name="conv_part",
    )(fields, conv_first, halo[0])
    w_qkv = pl.pallas_call(
        weights_kernel,
        out_shape=shape(w_qkv.shape, BF16),
        in_specs=[anywhere, anywhere],
        out_specs=vmem,
        scratch_shapes=[pltpu.SemaphoreType.DMA],
        compiler_params=pltpu.CompilerParams(vmem_limit_bytes=VMEM_LIMIT),
        cost_estimate=pl.CostEstimate(flops=int(2e9), bytes_accessed=0, transcendentals=0),
        name="weights_near",
    )(halo[0], w_qkv)
    flat = shape((tokens, width), BF16)
    stream, normed = call(
        functools.partial(first_kernel, dims), (flat, flat), (here,), (*part, *halo), [full], "conv_first", 2
    )

    forward = [(order[i], order[(i + 1) % lon_total]) for i in range(lon_total)]
    backward = [(b, a) for a, b in forward]
    state_shape = (shape((tokens, width), F32),) * 3
    handed, query, *state = call(
        functools.partial(own_kernel, factor),
        (flat, shape((pairs, 2 * tokens, LANES), BF16), *state_shape),
        (),
        (normed, w_qkv),
        [],
        "own_block",
        4,
    )

    def batch(state, waiting):
        blocks, slots = zip(*waiting)
        sizes = [b.shape[0] for b in blocks]
        return call(
            functools.partial(batch_kernel, factor, slots, sizes),
            state_shape,
            links,
            (query, w_qkv, *state, *blocks),
            [],
            "attend_batch",
            1 + 1.8 * len(blocks),
        )

    ahead, behind = normed, normed
    near = [(shift(handed, "lat", 1), ABOVE), (shift(handed, "lat", -1), BELOW)]
    waiting = []
    cut = (tokens // 32) * 16
    for step in range(1, half):
        ahead = lax.ppermute(ahead, "lon", forward)
        behind = lax.ppermute(behind, "lon", backward)
        if step > 1:
            state = batch(state, waiting)
        waiting = [(ahead, 2 * step - 2), (behind, 2 * step - 1), *near[step - 1 : step]]
    far_first = lax.ppermute(ahead[:cut], "lon", forward)
    far_second = lax.ppermute(behind[cut:], "lon", backward)
    state = batch(state, waiting)

    row_edge, column_edge = shape((levels, columns, width), BF16), shape((levels, rows, width), BF16)
    dense, after, *edges = call(
        functools.partial(last_kernel, factor, dims, [lon_total - 2] * 2, [cut, tokens - cut]),
        (shape((tokens, width), F32), part_shape[0], row_edge, row_edge, column_edge, column_edge),
        links,
        (query, w_qkv, *state, w_out, stream, far_first, far_second),
        [pltpu.VMEM((tokens, width), F32)],
        "attend_last",
        5,
    )
    halo = exchange(*edges, here)
    grid4 = shape(fields.shape, BF16)
    *part, attended = call(
        functools.partial(second_part_kernel, dims),
        (*part_shape, grid4),
        (),
        (after, conv_second, dense),
        [],
        "conv_part",
        2,
    )
    mixed = call(functools.partial(second_kernel, dims), grid4, (here,), (*part, *halo), [full], "conv_second", 2)
    return attended.transpose(0, 2, 1, 3), mixed.transpose(0, 2, 1, 3)


def solution(mesh):
    return jax.shard_map(
        local,
        mesh=mesh,
        in_specs=(
            P(None, "lat", "lon", None),
            P(),
            P(),
            P(),
            P(),
            P("lat", "lon", None),
            P("lat", "lon"),
        ),
        out_specs=(P(None, "lat", "lon", None), P(None, "lat", "lon", None)),
        check_vma=False,
    )
```

```python
import functools

import jax
import jax.numpy as jnp
import numpy as np
from jax import lax
from jax.experimental import pallas as pl
from jax.experimental.pallas import tpu as pltpu
from jax.sharding import PartitionSpec as P

HEADS = 16
EPSILON = 1e-05
MASKED = -1e30
LANES = 128
SUBLANES = 8
GROUP = 256
F32 = jnp.float32
BF16 = jnp.bfloat16
VMEM_LIMIT = 16 * 1024 * 1024
ABOVE, BELOW, OWN = -1, -2, -3


def ring_order(count):
    columns = 1
    while columns * columns * 4 <= count:
        columns *= 2
    rows = count // columns
    order = [z * columns for z in range(rows)]
    for turn, z in enumerate(range(rows - 1, -1, -1)):
        ys = list(range(1, columns))
        if turn % 2:
            ys.reverse()
        order += [z * columns + y for y in ys]
    return order


def shift(x, axis, by):
    size = lax.axis_size(axis)
    return lax.ppermute(x, axis, [(i, (i + by) % size) for i in range(size)])


def place(dims, level, column):
    levels, columns, rows = dims
    inner = columns - 2
    if 0 < column <= inner:
        return (level * inner + column - 1) * rows
    return (levels * inner + level * 2 + (column > 0)) * rows


def conv_part(load, dims, weights_ref, part_ref, taps_ref):
    levels, columns, rows = dims
    above = lax.broadcasted_iota(jnp.int32, (SUBLANES, LANES), 0) > 0
    blank = jnp.zeros((SUBLANES - rows, LANES), F32)
    nothing = jnp.zeros((SUBLANES, LANES), F32)

    def tile(index, carry):
        lanes = pl.ds(pl.multiple_of(index * LANES, LANES), LANES)
        taps_ref[index] = weights_ref[:, lanes]
        taps = [jnp.broadcast_to(weights_ref[k : k + 1, lanes], (SUBLANES, LANES)) for k in range(9)]
        for level in range(levels):
            strip = [jnp.concatenate([load(level, column, index, lanes), blank], axis=0) for column in range(columns)]
            strip = [nothing, *strip, nothing]
            for column in range(columns):
                near = strip[column : column + 3]
                sums = [taps[3 * a] * near[0] + taps[3 * a + 1] * near[1] + taps[3 * a + 2] * near[2] for a in range(3)]
                value = near[1] + sums[1]
                value += jnp.where(above, pltpu.roll(sums[0], 1, 0), 0.0)
                value += pltpu.roll(sums[2], SUBLANES - 1, 0)
                at = place(dims, level, column)
                part_ref[index, at : at + rows, :] = value[0:rows]
        return carry

    lax.fori_loop(0, part_ref.shape[0], tile, 0)


def first_part_kernel(field_ref, weights_ref, part_ref, taps_ref):
    levels, columns, rows, _ = field_ref.shape
    load = lambda level, column, index, lanes: field_ref[level, column, :, lanes].astype(F32)
    conv_part(load, (levels, columns, rows), weights_ref, part_ref, taps_ref)


def weights_kernel(inner_ref, far_ref, passed_ref, near_ref, arrived):
    copy = pltpu.make_async_copy(far_ref, near_ref, arrived)
    copy.start()
    passed_ref[...] = inner_ref[...]
    copy.wait()


def second_part_kernel(dims, field_ref, weights_ref, dense_ref, part_ref, taps_ref, attended_ref):
    levels, columns, rows = dims

    def load(level, column, index, lanes):
        at = place(dims, level, column)
        return field_ref[index, at : at + rows, :]

    conv_part(load, dims, weights_ref, part_ref, taps_ref)
    for level in range(levels):
        for column in range(columns):
            at = place(dims, level, column)
            attended_ref[level, column] = dense_ref[at : at + rows, :].astype(BF16)


def add_rows(index, dims, here_ref, north_ref, south_ref, taps_ref, full, inner_at, edge_at):
    levels, columns, rows = dims
    inner = columns - 2
    lanes = slice(index * LANES, (index + 1) * LANES)
    blank = jnp.zeros((1, LANES), F32)
    for level in range(levels):
        for ref, flag, a, row in ((north_ref, 0, 0, 0), (south_ref, 1, 2, rows - 1)):
            line = ref[level, :, lanes].astype(F32)
            if line.shape[0] == columns:
                line = jnp.concatenate([blank, line, blank], axis=0)
            left, line, right = (line[b : b + columns] for b in range(3))
            tap = [taps_ref[index, 3 * a + b : 3 * a + b + 1, :] for b in range(3)]
            more = tap[0] * left + tap[1] * line + tap[2] * right
            more = jnp.where(here_ref[flag] > 0, more, 0.0)
            if inner_at is not None:
                full[index, pl.ds(inner_at + level * inner * rows + row, inner, stride=rows), :] += more[1 : columns - 1]
            if edge_at is not None:
                ends = jnp.concatenate([more[:1], more[columns - 1 :]], axis=0)
                full[index, pl.ds(edge_at + level * 2 * rows + row, 2, stride=rows), :] += ends


def add_sides(index, dims, here_ref, across_ref, pair_ref, taps_ref, full, edge_at):
    levels, columns, rows = dims
    lanes = slice(index * LANES, (index + 1) * LANES)
    even = here_ref[2] > 0
    blank = jnp.zeros((1, LANES), F32)
    for level in range(levels):
        pair = pair_ref[level, :, lanes].astype(F32)
        across = across_ref[level, :, lanes].astype(F32)
        west = jnp.where(even, across, pair)
        east = jnp.where(even, pair, across)
        for side, b, order in ((west, 0, 0), (east, 2, 1)):
            if side.shape[0] == rows:
                side = jnp.concatenate([blank, side, blank], axis=0)
            more = None
            for a in range(3):
                term = taps_ref[index, 3 * a + b : 3 * a + b + 1, :] * side[a : a + rows]
                more = term if more is None else more + term
            at = edge_at + (level * 2 + order) * rows
            full[index, at : at + rows, :] += more


def normalise(full, stream_ref, put):
    tiles, tokens, _ = full.shape
    squares = jnp.zeros((tokens, LANES), F32)
    for index in range(tiles):
        stream = full[index].astype(BF16)
        stream_ref[:, index * LANES : (index + 1) * LANES] = stream
        wide = stream.astype(F32)
        squares += wide * wide
    mean = jnp.sum(squares, axis=-1, keepdims=True) * (1.0 / (tiles * LANES))
    scale = jnp.broadcast_to(lax.rsqrt(mean + EPSILON), (tokens, LANES))
    for index in range(tiles):
        lanes = slice(index * LANES, (index + 1) * LANES)
        put(lanes, (stream_ref[:, lanes].astype(F32) * scale).astype(BF16))


def inner_kernel(
    dims, here_ref, part_ref, taps_ref, north_ref, south_ref, west_ref, east_ref,
    stream_ref, normed_ref, across_ref, pair_ref, full,
):
    levels, columns, rows = dims
    tiles, tokens, _ = full.shape
    for index in range(tiles):
        full[index] = part_ref[index, 0:tokens, :]
        add_rows(index, dims, here_ref, north_ref, south_ref, taps_ref, full, 0, None)

    def put(lanes, value):
        normed_ref[:, lanes] = value

    normalise(full, stream_ref, put)
    has_north = (here_ref[0] > 0).astype(F32)
    has_south = (here_ref[1] > 0).astype(F32)
    even = here_ref[2] > 0
    for level in range(levels):
        north = north_ref[level].astype(F32) * has_north
        south = south_ref[level].astype(F32) * has_south
        tall = []
        for edge_ref, at in ((west_ref, 0), (east_ref, columns - 1)):
            middle = edge_ref[level].astype(F32)
            tall.append(jnp.concatenate([north[at : at + 1], middle, south[at : at + 1]], axis=0))
        across_ref[level] = jnp.where(even, tall[0], tall[1]).astype(BF16)
        pair_ref[level] = jnp.where(even, tall[1], tall[0]).astype(BF16)


def edge_kernel(
    dims, here_ref, part_ref, taps_ref, north_ref, south_ref, across_ref, pair_ref, inner_ref, ahead_ref, behind_ref,
    stream_ref, edge_ref, normed_ref, ahead_joined, behind_joined, full,
):
    tiles, tokens, _ = full.shape
    start = part_ref.shape[1] - tokens
    normed_ref[0:start, :] = inner_ref[...]
    ahead_joined[0:start, :] = ahead_ref[...]
    behind_joined[0:start, :] = behind_ref[...]
    for index in range(tiles):
        full[index] = part_ref[index, start : start + tokens, :]
        add_rows(index, dims, here_ref, north_ref, south_ref, taps_ref, full, None, 0)
        add_sides(index, dims, here_ref, across_ref, pair_ref, taps_ref, full, 0)

    def put(lanes, value):
        edge_ref[:, lanes] = value
        for ref in (normed_ref, ahead_joined, behind_joined):
            ref[start : start + tokens, lanes] = value

    normalise(full, stream_ref, put)


def second_kernel(dims, here_ref, part_ref, taps_ref, north_ref, south_ref, across_ref, pair_ref, mixed_ref, full):
    levels, columns, rows = dims
    edge_at = levels * (columns - 2) * rows
    for index in range(part_ref.shape[0]):
        lanes = slice(index * LANES, (index + 1) * LANES)
        full[index] = part_ref[index]
        add_rows(index, dims, here_ref, north_ref, south_ref, taps_ref, full, 0, edge_at)
        add_sides(index, dims, here_ref, across_ref, pair_ref, taps_ref, full, edge_at)
        for level in range(levels):
            for column in range(columns):
                at = place(dims, level, column)
                mixed_ref[level, column, :, lanes] = full[index, at : at + rows, :].astype(BF16)


def scores_of(query2, keys2, bias):
    scores = lax.dot_general(query2, keys2, (((1,), (1,)), ((), ())), preferred_element_type=F32)
    return scores if bias is None else scores + bias


def merge(both):
    half = both.shape[0] // 2
    low = lax.broadcasted_iota(jnp.int32, (half, LANES), 1) < LANES // 2
    return jnp.where(low, both[:half], both[half:])


def attend_pairs(factor, x, w_ref, bias, query_of, finish):
    width = x.shape[1]
    pairs = width // LANES
    inside = GROUP // LANES
    groups, scores = {}, {}

    def project(group):
        if group * GROUP < width and group not in groups:
            columns = lambda part: slice(part * width + group * GROUP, part * width + (group + 1) * GROUP)
            groups[group] = [
                jnp.dot(x, w_ref[:, columns(part)], preferred_element_type=F32).astype(BF16) for part in (1, 2)
            ]

    def lanes_of(pair):
        return slice(pair % inside * LANES, (pair % inside + 1) * LANES)

    def score(pair):
        if pair < pairs:
            project(pair // inside)
            scores[pair] = scores_of(query_of(pair), groups[pair // inside][0][:, lanes_of(pair)], bias)

    def weigh(pair, highest, weights):
        values2 = groups[pair // inside][1][:, lanes_of(pair)]
        beside = jnp.concatenate([values2, jnp.ones_like(values2)], axis=1)
        result = jnp.dot(weights, beside, preferred_element_type=F32)
        finish(pair, (merge(highest), merge(result[:, LANES:]), merge(result[:, :LANES])))

    score(0)
    waiting = None
    for pair in range(pairs):
        if (pair + 1) % inside == 1:
            project((pair + 1) // inside + 1)
        score(pair + 1)
        current = scores.pop(pair)
        highest = jnp.max(current, axis=-1, keepdims=True)
        weights = jnp.exp2((current - highest) * factor).astype(BF16)
        if waiting is not None:
            weigh(*waiting)
        waiting = (pair, highest, weights)
    weigh(*waiting)


def key_bias(here_ref, sources_ref, list_ref, count_ref, slots, sizes):
    lane = lax.broadcasted_iota(jnp.int32, (1, sum(sizes)), 1)
    bias = jnp.zeros((1, sum(sizes)), F32)
    count = count_ref[0, 0]
    start = 0
    for slot, size in zip(slots, sizes):
        if slot == OWN:
            start += size
            continue
        if slot == ABOVE:
            linked = here_ref[0]
        elif slot == BELOW:
            linked = here_ref[1]
        else:
            source = sources_ref[here_ref[3], slot]
            linked = jnp.int32(0)
            for entry in range(list_ref.shape[-1]):
                hit = (list_ref[0, 0, entry] == source) & (entry < count)
                linked = linked | hit.astype(jnp.int32)
        value = jnp.where(linked > 0, 0.0, MASKED).astype(F32)
        bias = jnp.where((lane >= start) & (lane < start + size), value, bias)
        start += size
    return bias


def joined(blocks):
    return blocks[0][...] if len(blocks) == 1 else jnp.concatenate([b[...] for b in blocks], axis=0)


def own_kernel(
    factor, slots, sizes, here_ref, sources_ref, list_ref, count_ref, x_ref, ahead_ref, behind_ref, w_ref,
    handed_ref, query_ref, high_ref, sum_ref, acc_ref,
):
    tokens, width = x_ref.shape
    x = x_ref[...]
    handed_ref[...] = x_ref[tokens - handed_ref.shape[0] :, :]
    bias = key_bias(here_ref, sources_ref, list_ref, count_ref, slots, sizes)
    low = lax.broadcasted_iota(jnp.int32, (tokens, LANES), 1) < LANES // 2
    zero = jnp.zeros((tokens, LANES), BF16)
    inside = GROUP // LANES
    queries = {}

    def query_of(pair):
        group = pair // inside
        if group not in queries:
            columns = slice(group * GROUP, (group + 1) * GROUP)
            queries[group] = jnp.dot(x, w_ref[:, columns], preferred_element_type=F32).astype(BF16)
        part = queries[group][:, pair % inside * LANES : (pair % inside + 1) * LANES]
        query2 = jnp.concatenate([jnp.where(low, part, zero), jnp.where(low, zero, part)], axis=0)
        query_ref[pair] = query2
        return query2

    def finish(pair, part):
        lanes = slice(pair * LANES, (pair + 1) * LANES)
        high_ref[:, lanes], sum_ref[:, lanes], acc_ref[:, lanes] = part

    attend_pairs(factor, joined([x_ref, ahead_ref, behind_ref]), w_ref, bias, query_of, finish)


def combine(state, part, factor):
    high = jnp.maximum(state[0], part[0])
    old = jnp.exp2((state[0] - high) * factor)
    new = jnp.exp2((part[0] - high) * factor)
    return high, state[1] * old + part[1] * new, state[2] * old + part[2] * new


def batch_kernel(
    factor, slots, sizes, here_ref, sources_ref, list_ref, count_ref, query_ref, w_ref, high_in, sum_in, acc_in, edge_ref, *refs
):
    blocks, (high_ref, sum_ref, acc_ref, handed_ref) = refs[:-4], refs[-4:]
    handed_ref[...] = edge_ref[...]
    bias = key_bias(here_ref, sources_ref, list_ref, count_ref, slots, sizes)

    def finish(pair, part):
        lanes = slice(pair * LANES, (pair + 1) * LANES)
        state = combine((high_in[:, lanes], sum_in[:, lanes], acc_in[:, lanes]), part, factor)
        high_ref[:, lanes], sum_ref[:, lanes], acc_ref[:, lanes] = state

    attend_pairs(factor, joined(blocks), w_ref, bias, lambda pair: query_ref[pair], finish)


def last_kernel(
    factor, dims, slots, sizes, here_ref, sources_ref, list_ref, count_ref, query_ref, w_ref, high_in, sum_in, acc_in,
    wo_ref, inner_ref, edge_ref, *refs
):
    blocks, (dense, after_ref, north_ref, south_ref, west_ref, east_ref, total) = refs[:-7], refs[-7:]
    levels, columns, rows = dims
    x = joined(blocks)
    width = x.shape[1]
    bias = key_bias(here_ref, sources_ref, list_ref, count_ref, slots, sizes)
    edge_at = inner_ref.shape[0]
    total[0:edge_at, :] = inner_ref[...].astype(F32)
    total[edge_at:, :] = edge_ref[...].astype(F32)

    def finish(pair, part):
        lanes = slice(pair * LANES, (pair + 1) * LANES)
        _, summed, result = combine((high_in[:, lanes], sum_in[:, lanes], acc_in[:, lanes]), part, factor)
        dense[:, lanes] = result / summed
        if (pair + 1) * LANES % GROUP == 0:
            chunk = slice((pair + 1) * LANES - GROUP, (pair + 1) * LANES)
            total[...] += jnp.dot(dense[:, chunk].astype(BF16), wo_ref[chunk, :], preferred_element_type=F32)

    attend_pairs(factor, x, w_ref, bias, lambda pair: query_ref[pair], finish)
    for index in range(width // LANES):
        lanes = slice(index * LANES, (index + 1) * LANES)
        after_ref[index] = total[:, lanes].astype(BF16).astype(F32)
        for level in range(levels):
            west_at = edge_at + level * 2 * rows
            east_at = west_at + rows
            for out_ref, row in ((north_ref, 0), (south_ref, rows - 1)):
                inner = after_ref[index, pl.ds(level * (columns - 2) * rows + row, columns - 2, stride=rows), :]
                west = after_ref[index, west_at + row : west_at + row + 1, :]
                east = after_ref[index, east_at + row : east_at + row + 1, :]
                out_ref[level, :, lanes] = jnp.concatenate([west, inner, east], axis=0).astype(BF16)
            west_ref[level, :, lanes] = after_ref[index, west_at : west_at + rows, :].astype(BF16)
            east_ref[level, :, lanes] = after_ref[index, east_at : east_at + rows, :].astype(BF16)


def shape(dims, kind):
    return jax.ShapeDtypeStruct(dims, kind)


def call(kernel, out_shape, scalars, arrays, scratch, name, microseconds, outside=()):
    return pl.pallas_call(
        kernel,
        out_shape=out_shape,
        in_specs=[pl.BlockSpec(memory_space=pltpu.SMEM)] * len(scalars) + [pl.BlockSpec(memory_space=pltpu.VMEM)] * len(arrays)
        + [pl.BlockSpec(memory_space=pl.ANY)] * len(outside),
        out_specs=jax.tree.map(lambda _: pl.BlockSpec(memory_space=pltpu.VMEM), out_shape),
        scratch_shapes=scratch,
        compiler_params=pltpu.CompilerParams(vmem_limit_bytes=VMEM_LIMIT),
        cost_estimate=pl.CostEstimate(flops=int(microseconds * 1.1e9), bytes_accessed=0, transcendentals=0),
        name=name,
    )(*scalars, *arrays, *outside)


def swap(value, first):
    count = lax.axis_size("lon")
    pairs = [p for i in range(first, count, 2) for p in ((i, (i + 1) % count), ((i + 1) % count, i))]
    return lax.ppermute(value, "lon", pairs)


def exchange(north_edge, south_edge, west_edge, east_edge, here):
    rows = west_edge.shape[1]
    even = here[2] > 0
    across = swap(jnp.where(even, west_edge, east_edge), 1)
    pair = swap(jnp.where(even, east_edge, west_edge), 0)
    west, east = jnp.where(even, across, pair), jnp.where(even, pair, across)

    def row(edge, at):
        return jnp.concatenate([west[:, at : at + 1], edge, east[:, at : at + 1]], axis=1)

    north = shift(row(south_edge, rows - 1), "lat", 1)
    south = shift(row(north_edge, 0), "lat", -1)
    return north, south, across, pair


def local(fields, conv_first, w_qkv, w_out, conv_second, key_list, key_count):
    fields = fields.transpose(0, 2, 1, 3)
    levels, columns, rows, width = fields.shape
    tokens = levels * rows * columns
    pairs = width // LANES
    factor = float(np.log2(np.e) * (width // HEADS) ** -0.5)
    lat_here = lax.axis_index("lat")
    lon_here = lax.axis_index("lon")
    lon_total = lax.axis_size("lon")
    order = ring_order(lon_total)
    place = {lon: i for i, lon in enumerate(order)}
    half = lon_total // 2
    table = np.zeros((lon_total, lon_total), np.int32)
    for lon in range(lon_total):
        for step in range(1, half + 1):
            table[lon, 2 * step - 2] = order[(place[lon] - step) % lon_total]
            table[lon, 2 * step - 1] = order[(place[lon] + step) % lon_total]
    here = jnp.stack(
        [lat_here > 0, lat_here < lax.axis_size("lat") - 1, lon_here % 2 == 0, lon_here]
    ).astype(jnp.int32)
    links = (here, jnp.asarray(table), key_list, key_count)

    dims = (levels, columns, rows)
    tiles = width // LANES
    edge_tokens = levels * 2 * rows
    inner_tokens = tokens - edge_tokens
    full = lambda count: pltpu.VMEM((tiles, count, LANES), F32)
    flat = lambda count: shape((count, width), BF16)
    part_shape = (shape((tiles, tokens, LANES), F32), shape((tiles, 9, LANES), F32))
    tall = shape((levels, rows + 2, width), BF16)
    forward = [(order[i], order[(i + 1) % lon_total]) for i in range(lon_total)]
    backward = [(b, a) for a, b in forward]

    north = shift(fields[:, :, rows - 1], "lat", 1)
    south = shift(fields[:, :, 0], "lat", -1)
    part = call(first_part_kernel, part_shape, (), (fields, conv_first), [], "conv_part", 1)
    stream_inner, normed_inner, across, pair = call(
        functools.partial(inner_kernel, dims),
        (flat(inner_tokens), flat(inner_tokens), tall, tall),
        (here,),
        (*part, north, south, fields[:, 0], fields[:, columns - 1]),
        [full(inner_tokens)],
        "conv_inner",
        1,
    )
    ahead = lax.ppermute(normed_inner, "lon", forward)
    behind = lax.ppermute(normed_inner, "lon", backward)
    across, pair = swap(across, 1), swap(pair, 0)
    anywhere = pl.BlockSpec(memory_space=pl.ANY)
    vmem = pl.BlockSpec(memory_space=pltpu.VMEM)
    normed_passed, w_qkv = pl.pallas_call(
        weights_kernel,
        out_shape=(flat(inner_tokens), shape(w_qkv.shape, BF16)),
        in_specs=[vmem, anywhere],
        out_specs=(vmem, vmem),
        scratch_shapes=[pltpu.SemaphoreType.DMA],
        compiler_params=pltpu.CompilerParams(vmem_limit_bytes=VMEM_LIMIT),
        cost_estimate=pl.CostEstimate(flops=int(2e9), bytes_accessed=0, transcendentals=0),
        name="weights_near",
    )(normed_inner, w_qkv)
    stream_edge, normed_edge, normed, *both = call(
        functools.partial(edge_kernel, dims),
        (flat(edge_tokens), flat(edge_tokens), flat(tokens), flat(tokens), flat(tokens)),
        (here,),
        (*part, north, south, across, pair, normed_inner, ahead, behind),
        [full(edge_tokens)],
        "conv_edge",
        1,
    )

    state_shape = (shape((tokens, width), F32),) * 3
    edge_passed, query, *state = call(
        functools.partial(own_kernel, factor, [OWN, 0, 1], [tokens, inner_tokens, inner_tokens]),
        (flat(edge_tokens), shape((pairs, 2 * tokens, LANES), BF16), *state_shape),
        links,
        (normed, ahead, behind, w_qkv),
        [],
        "own_block",
        4,
    )

    def batch(state, waiting):
        blocks = [block for block, _ in waiting]
        slots, sizes = zip(*[piece for _, pieces in waiting for piece in pieces])
        *state, handed = call(
            functools.partial(batch_kernel, factor, slots, sizes),
            (*state_shape, flat(edge_tokens)),
            links,
            (query, w_qkv, *state, normed_edge, *blocks),
            [],
            "attend_batch",
            1 + 1.2 * len(blocks),
        )
        return state, handed

    sides = ((ABOVE, 1), (BELOW, -1))
    near = {
        2: [(shift(normed_passed, "lat", by), [(slot, inner_tokens)]) for slot, by in sides],
        3: [(shift(edge_passed, "lat", by), [(slot, edge_tokens)]) for slot, by in sides],
    }
    ahead, behind = both
    handed = None
    for step in range(2, half):
        ahead = lax.ppermute(ahead, "lon", forward)
        behind = lax.ppermute(behind, "lon", backward)
        if step > 2:
            state, hand = batch(state, waiting)
            handed = hand if handed is None else handed
        waiting = [
            *near.get(step, ()),
            (ahead, [(2 * step - 2, inner_tokens), (2 * step - 4, edge_tokens)]),
            (behind, [(2 * step - 1, inner_tokens), (2 * step - 3, edge_tokens)]),
        ]
    last = lon_total - 2
    cut = (inner_tokens + 31) // 32 * 16
    far_first = lax.ppermute(jnp.concatenate([ahead[:cut], ahead[inner_tokens:]]), "lon", forward)
    far_second = lax.ppermute(behind[cut:], "lon", backward)
    state, _ = batch(state, waiting)
    far_edge = lax.ppermute(handed, "lon", [(order[i], order[(i + half) % lon_total]) for i in range(lon_total)])
    slots = [last, last - 2, last, last - 1, last]
    sizes = [cut, edge_tokens, inner_tokens - cut, edge_tokens, edge_tokens]

    row_edge, column_edge = shape((levels, columns, width), BF16), shape((levels, rows, width), BF16)
    dense, after, *edges = call(
        functools.partial(last_kernel, factor, dims, slots, sizes),
        (shape((tokens, width), F32), part_shape[0], row_edge, row_edge, column_edge, column_edge),
        links,
        (query, w_qkv, *state, w_out, stream_inner, stream_edge, far_first, far_second, far_edge),
        [pltpu.VMEM((tokens, width), F32)],
        "attend_last",
        5,
    )
    halo = exchange(*edges, here)
    grid4 = shape(fields.shape, BF16)
    *part, attended = call(
        functools.partial(second_part_kernel, dims),
        (*part_shape, grid4),
        (),
        (after, conv_second, dense),
        [],
        "conv_part",
        2,
    )
    mixed = call(functools.partial(second_kernel, dims), grid4, (here,), (*part, *halo), [full(tokens)], "conv_second", 2)
    return attended.transpose(0, 2, 1, 3), mixed.transpose(0, 2, 1, 3)


def solution(mesh):
    return jax.shard_map(
        local,
        mesh=mesh,
        in_specs=(
            P(None, "lat", "lon", None),
            P(),
            P(),
            P(),
            P(),
            P("lat", "lon", None),
            P("lat", "lon"),
        ),
        out_specs=(P(None, "lat", "lon", None), P(None, "lat", "lon", None)),
        check_vma=False,
    )
```

```python
import functools

import jax
import jax.numpy as jnp
import numpy as np
from jax import lax
from jax.experimental import pallas as pl
from jax.experimental.pallas import tpu as pltpu
from jax.sharding import PartitionSpec as P

HEADS = 16
EPSILON = 1e-05
MASKED = -1e30
LANES = 128
SUBLANES = 8
GROUP = 256
F32 = jnp.float32
BF16 = jnp.bfloat16
VMEM_LIMIT = 16 * 1024 * 1024
ABOVE, BELOW, OWN = -1, -2, -3


def ring_order(count):
    columns = 1
    while columns * columns * 4 <= count:
        columns *= 2
    rows = count // columns
    order = [z * columns for z in range(rows)]
    for turn, z in enumerate(range(rows - 1, -1, -1)):
        ys = list(range(1, columns))
        if turn % 2:
            ys.reverse()
        order += [z * columns + y for y in ys]
    return order


def shift(x, axis, by):
    size = lax.axis_size(axis)
    return lax.ppermute(x, axis, [(i, (i + by) % size) for i in range(size)])


def place(dims, level, column):
    levels, columns, rows = dims
    inner = columns - 2
    if 0 < column <= inner:
        return (level * inner + column - 1) * rows
    return (levels * inner + level * 2 + (column > 0)) * rows


def conv_part(load, dims, weights_ref, part_ref, taps_ref):
    levels, columns, rows = dims
    above = lax.broadcasted_iota(jnp.int32, (SUBLANES, LANES), 0) > 0
    blank = jnp.zeros((SUBLANES - rows, LANES), F32)
    nothing = jnp.zeros((SUBLANES, LANES), F32)

    def tile(index, carry):
        lanes = pl.ds(pl.multiple_of(index * LANES, LANES), LANES)
        taps_ref[index] = weights_ref[:, lanes]
        taps = [jnp.broadcast_to(weights_ref[k : k + 1, lanes], (SUBLANES, LANES)) for k in range(9)]
        for level in range(levels):
            strip = [jnp.concatenate([load(level, column, index, lanes), blank], axis=0) for column in range(columns)]
            strip = [nothing, *strip, nothing]
            for column in range(columns):
                near = strip[column : column + 3]
                sums = [taps[3 * a] * near[0] + taps[3 * a + 1] * near[1] + taps[3 * a + 2] * near[2] for a in range(3)]
                value = near[1] + sums[1]
                value += jnp.where(above, pltpu.roll(sums[0], 1, 0), 0.0)
                value += pltpu.roll(sums[2], SUBLANES - 1, 0)
                at = place(dims, level, column)
                part_ref[index, at : at + rows, :] = value[0:rows]
        return carry

    lax.fori_loop(0, part_ref.shape[0], tile, 0)


def first_part_kernel(field_ref, weights_ref, part_ref, taps_ref):
    levels, columns, rows, _ = field_ref.shape
    load = lambda level, column, index, lanes: field_ref[level, column, :, lanes].astype(F32)
    conv_part(load, (levels, columns, rows), weights_ref, part_ref, taps_ref)


def weights_kernel(inner_ref, far_ref, passed_ref, near_ref, arrived):
    copy = pltpu.make_async_copy(far_ref, near_ref, arrived)
    copy.start()
    passed_ref[...] = inner_ref[...]
    copy.wait()


def second_part_kernel(dims, field_ref, weights_ref, dense_ref, part_ref, taps_ref, attended_ref):
    levels, columns, rows = dims

    def load(level, column, index, lanes):
        at = place(dims, level, column)
        return field_ref[index, at : at + rows, :]

    conv_part(load, dims, weights_ref, part_ref, taps_ref)
    for level in range(levels):
        for column in range(columns):
            at = place(dims, level, column)
            attended_ref[level, column] = dense_ref[at : at + rows, :].astype(BF16)


def add_rows(index, dims, here_ref, north_ref, south_ref, taps_ref, full, inner_at, edge_at):
    levels, columns, rows = dims
    inner = columns - 2
    lanes = slice(index * LANES, (index + 1) * LANES)
    blank = jnp.zeros((1, LANES), F32)
    count = levels * columns
    for ref, flag, a, row in ((north_ref, 0, 0, 0), (south_ref, 1, 2, rows - 1)):
        lines = ref[:, lanes].astype(F32)
        for level in range(levels):
            ends = [blank, blank]
            if lines.shape[0] > count:
                ends = [lines[at : at + 1] for at in (count + level, count + levels + level)]
            line = jnp.concatenate([ends[0], lines[level * columns : (level + 1) * columns], ends[1]], axis=0)
            left, line, right = (line[b : b + columns] for b in range(3))
            tap = [taps_ref[index, 3 * a + b : 3 * a + b + 1, :] for b in range(3)]
            more = tap[0] * left + tap[1] * line + tap[2] * right
            more = jnp.where(here_ref[flag] > 0, more, 0.0)
            if inner_at is not None:
                full[index, pl.ds(inner_at + level * inner * rows + row, inner, stride=rows), :] += more[1 : columns - 1]
            if edge_at is not None:
                ends = jnp.concatenate([more[:1], more[columns - 1 :]], axis=0)
                full[index, pl.ds(edge_at + level * 2 * rows + row, 2, stride=rows), :] += ends


def add_sides(index, dims, here_ref, across_ref, pair_ref, taps_ref, full, edge_at):
    levels, columns, rows = dims
    lanes = slice(index * LANES, (index + 1) * LANES)
    even = here_ref[2] > 0
    blank = jnp.zeros((1, LANES), F32)
    for level in range(levels):
        pair = pair_ref[level, :, lanes].astype(F32)
        across = across_ref[level, :, lanes].astype(F32)
        west = jnp.where(even, across, pair)
        east = jnp.where(even, pair, across)
        for side, b, order in ((west, 0, 0), (east, 2, 1)):
            if side.shape[0] == rows:
                side = jnp.concatenate([blank, side, blank], axis=0)
            more = None
            for a in range(3):
                term = taps_ref[index, 3 * a + b : 3 * a + b + 1, :] * side[a : a + rows]
                more = term if more is None else more + term
            at = edge_at + (level * 2 + order) * rows
            full[index, at : at + rows, :] += more


def normalise(full, stream_ref, put):
    tiles, tokens, _ = full.shape
    squares = jnp.zeros((tokens, LANES), F32)
    for index in range(tiles):
        stream = full[index].astype(BF16)
        stream_ref[:, index * LANES : (index + 1) * LANES] = stream
        wide = stream.astype(F32)
        squares += wide * wide
    mean = jnp.sum(squares, axis=-1, keepdims=True) * (1.0 / (tiles * LANES))
    scale = jnp.broadcast_to(lax.rsqrt(mean + EPSILON), (tokens, LANES))
    for index in range(tiles):
        lanes = slice(index * LANES, (index + 1) * LANES)
        put(lanes, (stream_ref[:, lanes].astype(F32) * scale).astype(BF16))


def inner_kernel(
    dims, here_ref, part_ref, taps_ref, north_ref, south_ref, west_ref, east_ref,
    stream_ref, normed_ref, across_ref, pair_ref, even_ref, full,
):
    levels, columns, rows = dims
    tiles, tokens, _ = full.shape
    for index in range(tiles):
        full[index] = part_ref[index, 0:tokens, :]
        add_rows(index, dims, here_ref, north_ref, south_ref, taps_ref, full, 0, None)

    def put(lanes, value):
        normed_ref[:, lanes] = value

    normalise(full, stream_ref, put)
    even_ref[...] = jnp.full(even_ref.shape, here_ref[2], jnp.int32)
    has_north = (here_ref[0] > 0).astype(F32)
    has_south = (here_ref[1] > 0).astype(F32)
    even = here_ref[2] > 0
    north = north_ref[...].astype(F32) * has_north
    south = south_ref[...].astype(F32) * has_south
    for level in range(levels):
        tall = []
        for edge_ref, column in ((west_ref, 0), (east_ref, columns - 1)):
            middle = edge_ref[level].astype(F32)
            at = level * columns + column
            tall.append(jnp.concatenate([north[at : at + 1], middle, south[at : at + 1]], axis=0))
        across_ref[level] = jnp.where(even, tall[0], tall[1]).astype(BF16)
        pair_ref[level] = jnp.where(even, tall[1], tall[0]).astype(BF16)


def edge_kernel(
    dims, here_ref, part_ref, taps_ref, north_ref, south_ref, across_ref, pair_ref, inner_ref, ahead_ref, behind_ref,
    stream_ref, edge_ref, normed_ref, ahead_joined, behind_joined, full,
):
    tiles, tokens, _ = full.shape
    start = part_ref.shape[1] - tokens
    normed_ref[0:start, :] = inner_ref[...]
    ahead_joined[0:start, :] = ahead_ref[...]
    behind_joined[0:start, :] = behind_ref[...]
    for index in range(tiles):
        full[index] = part_ref[index, start : start + tokens, :]
        add_rows(index, dims, here_ref, north_ref, south_ref, taps_ref, full, None, 0)
        add_sides(index, dims, here_ref, across_ref, pair_ref, taps_ref, full, 0)

    def put(lanes, value):
        edge_ref[:, lanes] = value
        for ref in (normed_ref, ahead_joined, behind_joined):
            ref[start : start + tokens, lanes] = value

    normalise(full, stream_ref, put)


def second_kernel(dims, here_ref, part_ref, taps_ref, north_ref, south_ref, across_ref, pair_ref, mixed_ref, full):
    levels, columns, rows = dims
    edge_at = levels * (columns - 2) * rows
    for index in range(part_ref.shape[0]):
        lanes = slice(index * LANES, (index + 1) * LANES)
        full[index] = part_ref[index]
        add_rows(index, dims, here_ref, north_ref, south_ref, taps_ref, full, 0, edge_at)
        add_sides(index, dims, here_ref, across_ref, pair_ref, taps_ref, full, edge_at)
        for level in range(levels):
            for column in range(columns):
                at = place(dims, level, column)
                mixed_ref[level, column, :, lanes] = full[index, at : at + rows, :].astype(BF16)


def scores_of(query2, keys2, bias):
    scores = lax.dot_general(query2, keys2, (((1,), (1,)), ((), ())), preferred_element_type=F32)
    return scores if bias is None else scores + bias


def merge(both):
    half = both.shape[0] // 2
    low = lax.broadcasted_iota(jnp.int32, (half, LANES), 1) < LANES // 2
    return jnp.where(low, both[:half], both[half:])


def attend_pairs(factor, x, w_ref, bias, query_of, finish):
    width = x.shape[1]
    pairs = width // LANES
    inside = GROUP // LANES
    groups, scores = {}, {}

    def project(group):
        if group * GROUP < width and group not in groups:
            columns = lambda part: slice(part * width + group * GROUP, part * width + (group + 1) * GROUP)
            groups[group] = [
                jnp.dot(x, w_ref[:, columns(part)], preferred_element_type=F32).astype(BF16) for part in (1, 2)
            ]

    def lanes_of(pair):
        return slice(pair % inside * LANES, (pair % inside + 1) * LANES)

    def score(pair):
        if pair < pairs:
            project(pair // inside)
            scores[pair] = scores_of(query_of(pair), groups[pair // inside][0][:, lanes_of(pair)], bias)

    def weigh(pair, highest, weights):
        values2 = groups[pair // inside][1][:, lanes_of(pair)]
        beside = jnp.concatenate([values2, jnp.ones_like(values2)], axis=1)
        result = jnp.dot(weights, beside, preferred_element_type=F32)
        finish(pair, (merge(highest), merge(result[:, LANES:]), merge(result[:, :LANES])))

    score(0)
    waiting = None
    for pair in range(pairs):
        if (pair + 1) % inside == 1:
            project((pair + 1) // inside + 1)
        score(pair + 1)
        current = scores.pop(pair)
        highest = jnp.max(current, axis=-1, keepdims=True)
        weights = jnp.exp2((current - highest) * factor).astype(BF16)
        if waiting is not None:
            weigh(*waiting)
        waiting = (pair, highest, weights)
    weigh(*waiting)


def key_bias(here_ref, sources_ref, list_ref, count_ref, slots, sizes):
    lane = lax.broadcasted_iota(jnp.int32, (1, sum(sizes)), 1)
    bias = jnp.zeros((1, sum(sizes)), F32)
    count = count_ref[0, 0]
    start = 0
    for slot, size in zip(slots, sizes):
        if slot == OWN:
            start += size
            continue
        if slot == ABOVE:
            linked = here_ref[0]
        elif slot == BELOW:
            linked = here_ref[1]
        else:
            source = sources_ref[here_ref[3], slot]
            linked = jnp.int32(0)
            for entry in range(list_ref.shape[-1]):
                hit = (list_ref[0, 0, entry] == source) & (entry < count)
                linked = linked | hit.astype(jnp.int32)
        value = jnp.where(linked > 0, 0.0, MASKED).astype(F32)
        bias = jnp.where((lane >= start) & (lane < start + size), value, bias)
        start += size
    return bias


def joined(blocks):
    return blocks[0][...] if len(blocks) == 1 else jnp.concatenate([b[...] for b in blocks], axis=0)


def own_kernel(
    factor, slots, sizes, here_ref, sources_ref, list_ref, count_ref, x_ref, ahead_ref, behind_ref, w_ref,
    handed_ref, query_ref, high_ref, sum_ref, acc_ref,
):
    tokens, width = x_ref.shape
    x = x_ref[...]
    handed_ref[...] = x_ref[tokens - handed_ref.shape[0] :, :]
    bias = key_bias(here_ref, sources_ref, list_ref, count_ref, slots, sizes)
    low = lax.broadcasted_iota(jnp.int32, (tokens, LANES), 1) < LANES // 2
    zero = jnp.zeros((tokens, LANES), BF16)
    inside = GROUP // LANES
    queries = {}

    def query_of(pair):
        group = pair // inside
        if group not in queries:
            columns = slice(group * GROUP, (group + 1) * GROUP)
            queries[group] = jnp.dot(x, w_ref[:, columns], preferred_element_type=F32).astype(BF16)
        part = queries[group][:, pair % inside * LANES : (pair % inside + 1) * LANES]
        query2 = jnp.concatenate([jnp.where(low, part, zero), jnp.where(low, zero, part)], axis=0)
        query_ref[pair] = query2
        return query2

    def finish(pair, part):
        lanes = slice(pair * LANES, (pair + 1) * LANES)
        high_ref[:, lanes], sum_ref[:, lanes], acc_ref[:, lanes] = part

    seen = joined([x_ref, ahead_ref, behind_ref])
    attend_pairs(factor, seen, w_ref, bias, query_of, finish)


def combine(state, part, factor):
    high = jnp.maximum(state[0], part[0])
    old = jnp.exp2((state[0] - high) * factor)
    new = jnp.exp2((part[0] - high) * factor)
    return high, state[1] * old + part[1] * new, state[2] * old + part[2] * new


def batch_kernel(
    factor, slots, sizes, here_ref, sources_ref, list_ref, count_ref, query_ref, w_ref, high_in, sum_in, acc_in, edge_ref, *refs
):
    blocks, (high_ref, sum_ref, acc_ref, handed_ref) = refs[:-4], refs[-4:]
    handed_ref[...] = edge_ref[...]
    bias = key_bias(here_ref, sources_ref, list_ref, count_ref, slots, sizes)

    def finish(pair, part):
        lanes = slice(pair * LANES, (pair + 1) * LANES)
        state = combine((high_in[:, lanes], sum_in[:, lanes], acc_in[:, lanes]), part, factor)
        high_ref[:, lanes], sum_ref[:, lanes], acc_ref[:, lanes] = state

    attend_pairs(factor, joined(blocks), w_ref, bias, lambda pair: query_ref[pair], finish)


def last_kernel(
    factor, dims, slots, sizes, here_ref, sources_ref, list_ref, count_ref, query_ref, w_ref, high_in, sum_in, acc_in,
    wo_ref, inner_ref, edge_ref, *refs
):
    blocks, (dense, after_ref, north_ref, south_ref, across_ref, pair_ref, total) = refs[:-7], refs[-7:]
    levels, columns, rows = dims
    x = joined(blocks)
    width = x.shape[1]
    bias = key_bias(here_ref, sources_ref, list_ref, count_ref, slots, sizes)
    edge_at = inner_ref.shape[0]
    total[0:edge_at, :] = inner_ref[...].astype(F32)
    total[edge_at:, :] = edge_ref[...].astype(F32)

    def finish(pair, part):
        lanes = slice(pair * LANES, (pair + 1) * LANES)
        _, summed, result = combine((high_in[:, lanes], sum_in[:, lanes], acc_in[:, lanes]), part, factor)
        dense[:, lanes] = result / summed
        if (pair + 1) * LANES % GROUP == 0:
            chunk = slice((pair + 1) * LANES - GROUP, (pair + 1) * LANES)
            total[...] += jnp.dot(dense[:, chunk].astype(BF16), wo_ref[chunk, :], preferred_element_type=F32)

    attend_pairs(factor, x, w_ref, bias, lambda pair: query_ref[pair], finish)
    for index in range(width // LANES):
        lanes = slice(index * LANES, (index + 1) * LANES)
        after_ref[index] = total[:, lanes].astype(BF16).astype(F32)
        for out_ref, row in ((north_ref, 0), (south_ref, rows - 1)):
            pieces = []
            for level in range(levels):
                west_at = edge_at + level * 2 * rows + row
                inner = after_ref[index, pl.ds(level * (columns - 2) * rows + row, columns - 2, stride=rows), :]
                pieces += [after_ref[index, west_at : west_at + 1, :], inner]
                pieces += [after_ref[index, west_at + rows : west_at + rows + 1, :]]
            out_ref[:, lanes] = jnp.concatenate(pieces, axis=0).astype(BF16)
        for level in range(levels):
            west_at = edge_at + level * 2 * rows
            east_at = west_at + rows
            west = after_ref[index, west_at : west_at + rows, :]
            east = after_ref[index, east_at : east_at + rows, :]
            across_ref[level, :, lanes] = jnp.where(here_ref[2] > 0, west, east).astype(BF16)
            pair_ref[level, :, lanes] = jnp.where(here_ref[2] > 0, east, west).astype(BF16)


def shape(dims, kind):
    return jax.ShapeDtypeStruct(dims, kind)


def call(kernel, out_shape, scalars, arrays, scratch, name, microseconds, outside=()):
    return pl.pallas_call(
        kernel,
        out_shape=out_shape,
        in_specs=[pl.BlockSpec(memory_space=pltpu.SMEM)] * len(scalars) + [pl.BlockSpec(memory_space=pltpu.VMEM)] * len(arrays)
        + [pl.BlockSpec(memory_space=pl.ANY)] * len(outside),
        out_specs=jax.tree.map(lambda _: pl.BlockSpec(memory_space=pltpu.VMEM), out_shape),
        scratch_shapes=scratch,
        compiler_params=pltpu.CompilerParams(vmem_limit_bytes=VMEM_LIMIT),
        cost_estimate=pl.CostEstimate(flops=int(microseconds * 1.1e9), bytes_accessed=0, transcendentals=0),
        name=name,
    )(*scalars, *arrays, *outside)


def swap(value, first):
    count = lax.axis_size("lon")
    pairs = [p for i in range(first, count, 2) for p in ((i, (i + 1) % count), ((i + 1) % count, i))]
    return lax.ppermute(value, "lon", pairs)


def exchange(north_edge, south_edge, across, pair, even):
    rows = across.shape[1]
    across, pair = swap(across, 1), swap(pair, 0)
    even = even[None] > 0
    west, east = jnp.where(even, across, pair), jnp.where(even, pair, across)

    def row(edge, at):
        return jnp.concatenate([edge, west[:, at], east[:, at]], axis=0)

    north = shift(row(south_edge, rows - 1), "lat", 1)
    south = shift(row(north_edge, 0), "lat", -1)
    return north, south, across, pair


def local(fields, conv_first, w_qkv, w_out, conv_second, key_list, key_count):
    fields = fields.transpose(0, 2, 1, 3)
    levels, columns, rows, width = fields.shape
    tokens = levels * rows * columns
    pairs = width // LANES
    factor = float(np.log2(np.e) * (width // HEADS) ** -0.5)
    lat_here = lax.axis_index("lat")
    lon_here = lax.axis_index("lon")
    lon_total = lax.axis_size("lon")
    order = ring_order(lon_total)
    place = {lon: i for i, lon in enumerate(order)}
    half = lon_total // 2
    table = np.zeros((lon_total, lon_total), np.int32)
    for lon in range(lon_total):
        for step in range(1, half + 1):
            table[lon, 2 * step - 2] = order[(place[lon] - step) % lon_total]
            table[lon, 2 * step - 1] = order[(place[lon] + step) % lon_total]
    here = jnp.stack(
        [lat_here > 0, lat_here < lax.axis_size("lat") - 1, lon_here % 2 == 0, lon_here]
    ).astype(jnp.int32)
    links = (here, jnp.asarray(table), key_list, key_count)

    dims = (levels, columns, rows)
    tiles = width // LANES
    edge_tokens = levels * 2 * rows
    inner_tokens = tokens - edge_tokens
    full = lambda count: pltpu.VMEM((tiles, count, LANES), F32)
    flat = lambda count: shape((count, width), BF16)
    part_shape = (shape((tiles, tokens, LANES), F32), shape((tiles, 9, LANES), F32))
    tall = shape((levels, rows + 2, width), BF16)
    forward = [(order[i], order[(i + 1) % lon_total]) for i in range(lon_total)]
    backward = [(b, a) for a, b in forward]

    north = shift(fields[:, :, rows - 1].reshape(levels * columns, width), "lat", 1)
    south = shift(fields[:, :, 0].reshape(levels * columns, width), "lat", -1)
    part = call(first_part_kernel, part_shape, (), (fields, conv_first), [], "conv_part", 1)
    stream_inner, normed_inner, across, pair, even = call(
        functools.partial(inner_kernel, dims),
        (flat(inner_tokens), flat(inner_tokens), tall, tall, shape((1, width), jnp.int32)),
        (here,),
        (*part, north, south, fields[:, 0], fields[:, columns - 1]),
        [full(inner_tokens)],
        "conv_inner",
        1,
    )
    ahead = lax.ppermute(normed_inner, "lon", forward)
    behind = lax.ppermute(normed_inner, "lon", backward)
    across, pair = swap(across, 1), swap(pair, 0)
    anywhere = pl.BlockSpec(memory_space=pl.ANY)
    vmem = pl.BlockSpec(memory_space=pltpu.VMEM)
    inner_passed, w_qkv = pl.pallas_call(
        weights_kernel,
        out_shape=(flat(inner_tokens), shape(w_qkv.shape, BF16)),
        in_specs=[vmem, anywhere],
        out_specs=(vmem, vmem),
        scratch_shapes=[pltpu.SemaphoreType.DMA],
        compiler_params=pltpu.CompilerParams(vmem_limit_bytes=VMEM_LIMIT),
        cost_estimate=pl.CostEstimate(flops=int(2e9), bytes_accessed=0, transcendentals=0),
        name="weights_near",
    )(normed_inner, w_qkv)
    stream_edge, normed_edge, normed, *both = call(
        functools.partial(edge_kernel, dims),
        (flat(edge_tokens), flat(edge_tokens), flat(tokens), flat(tokens), flat(tokens)),
        (here,),
        (*part, north, south, across, pair, normed_inner, ahead, behind),
        [full(edge_tokens)],
        "conv_edge",
        1,
    )

    state_shape = (shape((tokens, width), F32),) * 3
    edge_passed, query, *state = call(
        functools.partial(own_kernel, factor, [OWN, 0, 1], [tokens, inner_tokens, inner_tokens]),
        (flat(edge_tokens), shape((pairs, 2 * tokens, LANES), BF16), *state_shape),
        links,
        (normed, ahead, behind, w_qkv),
        [],
        "own_block",
        4,
    )

    def batch(state, waiting):
        blocks = [block for block, _ in waiting]
        slots, sizes = zip(*[piece for _, pieces in waiting for piece in pieces])
        *state, handed = call(
            functools.partial(batch_kernel, factor, slots, sizes),
            (*state_shape, flat(edge_tokens)),
            links,
            (query, w_qkv, *state, normed_edge, *blocks),
            [],
            "attend_batch",
            1 + 1.2 * len(blocks),
        )
        return state, handed

    sides = ((ABOVE, 1), (BELOW, -1))
    near = {
        2: [(shift(inner_passed, "lat", by), [(slot, inner_tokens)]) for slot, by in sides],
        3: [(shift(edge_passed, "lat", by), [(slot, edge_tokens)]) for slot, by in sides],
    }
    ahead, behind = both
    for step in range(2, half):
        ahead = lax.ppermute(ahead, "lon", forward)
        behind = lax.ppermute(behind, "lon", backward)
        if step > 2:
            state, handed = batch(state, waiting)
            if step == 3:
                opposite = [(order[i], order[(i + half) % lon_total]) for i in range(lon_total)]
                far_edge = lax.ppermute(handed, "lon", opposite)
        waiting = [
            (ahead, [(2 * step - 2, inner_tokens), (2 * step - 4, edge_tokens)]),
            (behind, [(2 * step - 1, inner_tokens), (2 * step - 3, edge_tokens)]),
            *near.get(step, ()),
        ]
    last = lon_total - 2
    cut = (inner_tokens + 31) // 32 * 16
    far_first = lax.ppermute(jnp.concatenate([ahead[:cut], ahead[inner_tokens:]]), "lon", forward)
    far_second = lax.ppermute(behind[cut:], "lon", backward)
    state, _ = batch(state, waiting)
    slots = [last, last - 2, last, last - 1, last]
    sizes = [cut, edge_tokens, inner_tokens - cut, edge_tokens, edge_tokens]

    row_edge, column_edge = flat(levels * columns), shape((levels, rows, width), BF16)
    dense, after, *edges = call(
        functools.partial(last_kernel, factor, dims, slots, sizes),
        (shape((tokens, width), F32), part_shape[0], row_edge, row_edge, column_edge, column_edge),
        links,
        (query, w_qkv, *state, w_out, stream_inner, stream_edge, far_first, far_second, far_edge),
        [pltpu.VMEM((tokens, width), F32)],
        "attend_last",
        5,
    )
    halo = exchange(*edges, even)
    grid4 = shape(fields.shape, BF16)
    *part, attended = call(
        functools.partial(second_part_kernel, dims),
        (*part_shape, grid4),
        (),
        (after, conv_second, dense),
        [],
        "conv_part",
        2,
    )
    mixed = call(functools.partial(second_kernel, dims), grid4, (here,), (*part, *halo), [full(tokens)], "conv_second", 2)
    return attended.transpose(0, 2, 1, 3), mixed.transpose(0, 2, 1, 3)


def solution(mesh):
    return jax.shard_map(
        local,
        mesh=mesh,
        in_specs=(
            P(None, "lat", "lon", None),
            P(),
            P(),
            P(),
            P(),
            P("lat", "lon", None),
            P("lat", "lon"),
        ),
        out_specs=(P(None, "lat", "lon", None), P(None, "lat", "lon", None)),
        check_vma=False,
    )
```

```python
import functools

import jax
import jax.numpy as jnp
import numpy as np
from jax import lax
from jax.experimental import pallas as pl
from jax.experimental.pallas import tpu as pltpu
from jax.sharding import PartitionSpec as P

HEADS = 16
EPSILON = 1e-05
MASKED = -1e30
LANES = 128
SUBLANES = 8
GROUP = 256
F32 = jnp.float32
BF16 = jnp.bfloat16
VMEM_LIMIT = 16 * 1024 * 1024
ABOVE, BELOW, OWN = -1, -2, -3


def ring_order(count):
    columns = 1
    while columns * columns * 4 <= count:
        columns *= 2
    rows = count // columns
    order = [z * columns for z in range(rows)]
    for turn, z in enumerate(range(rows - 1, -1, -1)):
        ys = list(range(1, columns))
        if turn % 2:
            ys.reverse()
        order += [z * columns + y for y in ys]
    return order


def shift(x, axis, by):
    size = lax.axis_size(axis)
    return lax.ppermute(x, axis, [(i, (i + by) % size) for i in range(size)])


def place(dims, level, column):
    levels, columns, rows = dims
    inner = columns - 2
    if 0 < column <= inner:
        return (level * inner + column - 1) * rows
    return (levels * inner + level * 2 + (column > 0)) * rows


def conv_part(load, dims, weights_ref, part_ref, taps_ref):
    levels, columns, rows = dims
    above = lax.broadcasted_iota(jnp.int32, (SUBLANES, LANES), 0) > 0
    blank = jnp.zeros((SUBLANES - rows, LANES), F32)
    nothing = jnp.zeros((SUBLANES, LANES), F32)

    def tile(index, carry):
        lanes = pl.ds(pl.multiple_of(index * LANES, LANES), LANES)
        taps_ref[index] = weights_ref[:, lanes]
        taps = [jnp.broadcast_to(weights_ref[k : k + 1, lanes], (SUBLANES, LANES)) for k in range(9)]
        for level in range(levels):
            strip = [jnp.concatenate([load(level, column, index, lanes), blank], axis=0) for column in range(columns)]
            strip = [nothing, *strip, nothing]
            for column in range(columns):
                near = strip[column : column + 3]
                sums = [taps[3 * a] * near[0] + taps[3 * a + 1] * near[1] + taps[3 * a + 2] * near[2] for a in range(3)]
                value = near[1] + sums[1]
                value += jnp.where(above, pltpu.roll(sums[0], 1, 0), 0.0)
                value += pltpu.roll(sums[2], SUBLANES - 1, 0)
                at = place(dims, level, column)
                part_ref[index, at : at + rows, :] = value[0:rows]
        return carry

    lax.fori_loop(0, part_ref.shape[0], tile, 0)


def rows_kernel(field_ref, north_ref, south_ref, near_ref, flat_ref):
    near_ref[...] = field_ref[...]
    levels, columns, rows, width = field_ref.shape
    count = levels * columns
    for index in range(width // LANES):
        lanes = slice(index * LANES, (index + 1) * LANES)
        for level in range(levels):
            for column in range(columns):
                at = (level * columns + column) * rows
                flat_ref[index, at : at + rows, :] = field_ref[level, column, :, lanes].astype(F32)
        north_ref[:, lanes] = flat_ref[index, pl.ds(0, count, stride=rows), :].astype(BF16)
        south_ref[:, lanes] = flat_ref[index, pl.ds(rows - 1, count, stride=rows), :].astype(BF16)


def first_part_kernel(field_ref, weights_ref, part_ref, taps_ref):
    levels, columns, rows, _ = field_ref.shape
    load = lambda level, column, index, lanes: field_ref[level, column, :, lanes].astype(F32)
    conv_part(load, (levels, columns, rows), weights_ref, part_ref, taps_ref)


def weights_kernel(inner_ref, far_ref, passed_ref, near_ref, arrived):
    copy = pltpu.make_async_copy(far_ref, near_ref, arrived)
    copy.start()
    passed_ref[...] = inner_ref[...]
    copy.wait()


def second_part_kernel(
    dims, here_ref, field_ref, weights_ref, dense_ref, across_ref, pair_ref, part_ref, taps_ref, attended_ref
):
    levels, columns, rows = dims

    def load(level, column, index, lanes):
        at = place(dims, level, column)
        return field_ref[index, at : at + rows, :]

    conv_part(load, dims, weights_ref, part_ref, taps_ref)
    for index in range(part_ref.shape[0]):
        add_sides(index, dims, here_ref, across_ref, pair_ref, taps_ref, part_ref, levels * (columns - 2) * rows)
    for level in range(levels):
        for column in range(columns):
            at = place(dims, level, column)
            attended_ref[level, column] = dense_ref[at : at + rows, :].astype(BF16)


def add_rows(index, dims, here_ref, north_ref, south_ref, taps_ref, full, inner_at, edge_at):
    levels, columns, rows = dims
    inner = columns - 2
    lanes = slice(index * LANES, (index + 1) * LANES)
    blank = jnp.zeros((1, LANES), F32)
    count = levels * columns
    for ref, flag, a, row in ((north_ref, 0, 0, 0), (south_ref, 1, 2, rows - 1)):
        lines = ref[:, lanes].astype(F32)
        for level in range(levels):
            ends = [blank, blank]
            if lines.shape[0] > count:
                ends = [lines[at : at + 1] for at in (count + level, count + levels + level)]
            line = jnp.concatenate([ends[0], lines[level * columns : (level + 1) * columns], ends[1]], axis=0)
            left, line, right = (line[b : b + columns] for b in range(3))
            tap = [taps_ref[index, 3 * a + b : 3 * a + b + 1, :] for b in range(3)]
            more = tap[0] * left + tap[1] * line + tap[2] * right
            more = jnp.where(here_ref[flag] > 0, more, 0.0)
            if inner_at is not None:
                full[index, pl.ds(inner_at + level * inner * rows + row, inner, stride=rows), :] += more[1 : columns - 1]
            if edge_at is not None:
                ends = jnp.concatenate([more[:1], more[columns - 1 :]], axis=0)
                full[index, pl.ds(edge_at + level * 2 * rows + row, 2, stride=rows), :] += ends


def add_sides(index, dims, here_ref, across_ref, pair_ref, taps_ref, full, edge_at):
    levels, columns, rows = dims
    lanes = slice(index * LANES, (index + 1) * LANES)
    even = here_ref[2] > 0
    blank = jnp.zeros((1, LANES), F32)
    pair = pair_ref[:, lanes].astype(F32)
    across = across_ref[:, lanes].astype(F32)
    both = jnp.where(even, across, pair), jnp.where(even, pair, across)
    tall = pair.shape[0] // levels
    for level in range(levels):
        west, east = (side[level * tall : (level + 1) * tall] for side in both)
        for side, b, order in ((west, 0, 0), (east, 2, 1)):
            if side.shape[0] == rows:
                side = jnp.concatenate([blank, side, blank], axis=0)
            more = None
            for a in range(3):
                term = taps_ref[index, 3 * a + b : 3 * a + b + 1, :] * side[a : a + rows]
                more = term if more is None else more + term
            at = edge_at + (level * 2 + order) * rows
            full[index, at : at + rows, :] += more


def normalise(full, stream_ref, put):
    tiles, tokens, _ = full.shape
    squares = jnp.zeros((tokens, LANES), F32)
    for index in range(tiles):
        stream = full[index].astype(BF16)
        stream_ref[:, index * LANES : (index + 1) * LANES] = stream
        wide = stream.astype(F32)
        squares += wide * wide
    mean = jnp.sum(squares, axis=-1, keepdims=True) * (1.0 / (tiles * LANES))
    scale = jnp.broadcast_to(lax.rsqrt(mean + EPSILON), (tokens, LANES))
    for index in range(tiles):
        lanes = slice(index * LANES, (index + 1) * LANES)
        put(lanes, (stream_ref[:, lanes].astype(F32) * scale).astype(BF16))


def inner_kernel(
    dims, here_ref, part_ref, taps_ref, north_ref, south_ref, field_ref,
    stream_ref, normed_ref, across_ref, pair_ref, even_ref, full,
):
    levels, columns, rows = dims
    tiles, tokens, _ = full.shape
    for index in range(tiles):
        full[index] = part_ref[index, 0:tokens, :]
        add_rows(index, dims, here_ref, north_ref, south_ref, taps_ref, full, 0, None)

    def put(lanes, value):
        normed_ref[:, lanes] = value

    normalise(full, stream_ref, put)
    even_ref[...] = jnp.full(even_ref.shape, here_ref[2], jnp.int32)
    has_north = (here_ref[0] > 0).astype(F32)
    has_south = (here_ref[1] > 0).astype(F32)
    even = here_ref[2] > 0
    north = north_ref[...].astype(F32) * has_north
    south = south_ref[...].astype(F32) * has_south
    tall = []
    for column in (0, columns - 1):
        pieces = []
        for level in range(levels):
            at = level * columns + column
            pieces += [north[at : at + 1], field_ref[level, column].astype(F32), south[at : at + 1]]
        tall.append(jnp.concatenate(pieces, axis=0))
    across_ref[...] = jnp.where(even, tall[0], tall[1]).astype(BF16)
    pair_ref[...] = jnp.where(even, tall[1], tall[0]).astype(BF16)


def edge_kernel(
    dims, here_ref, part_ref, taps_ref, north_ref, south_ref, across_ref, pair_ref, inner_ref, ahead_ref, behind_ref,
    stream_ref, edge_ref, normed_ref, ahead_joined, behind_joined, full,
):
    tiles, tokens, _ = full.shape
    start = part_ref.shape[1] - tokens
    normed_ref[0:start, :] = inner_ref[...]
    ahead_joined[0:start, :] = ahead_ref[...]
    behind_joined[0:start, :] = behind_ref[...]
    for index in range(tiles):
        full[index] = part_ref[index, start : start + tokens, :]
        add_rows(index, dims, here_ref, north_ref, south_ref, taps_ref, full, None, 0)
        add_sides(index, dims, here_ref, across_ref, pair_ref, taps_ref, full, 0)

    def put(lanes, value):
        edge_ref[:, lanes] = value
        for ref in (normed_ref, ahead_joined, behind_joined):
            ref[start : start + tokens, lanes] = value

    normalise(full, stream_ref, put)


def second_kernel(dims, here_ref, part_ref, taps_ref, north_ref, south_ref, mixed_ref, full):
    levels, columns, rows = dims
    edge_at = levels * (columns - 2) * rows
    for index in range(part_ref.shape[0]):
        lanes = slice(index * LANES, (index + 1) * LANES)
        full[index] = part_ref[index]
        add_rows(index, dims, here_ref, north_ref, south_ref, taps_ref, full, 0, edge_at)
        for level in range(levels):
            for column in range(columns):
                at = place(dims, level, column)
                mixed_ref[level, column, :, lanes] = full[index, at : at + rows, :].astype(BF16)


def scores_of(query2, keys2, bias):
    scores = lax.dot_general(query2, keys2, (((1,), (1,)), ((), ())), preferred_element_type=F32)
    return scores if bias is None else scores + bias


def merge(both):
    half = both.shape[0] // 2
    low = lax.broadcasted_iota(jnp.int32, (half, LANES), 1) < LANES // 2
    return jnp.where(low, both[:half], both[half:])


def attend_pairs(factor, x, w_ref, bias, query_of, finish):
    width = x.shape[1]
    pairs = width // LANES
    inside = GROUP // LANES
    groups, scores = {}, {}

    def project(group):
        if group * GROUP < width and group not in groups:
            columns = lambda part: slice(part * width + group * GROUP, part * width + (group + 1) * GROUP)
            groups[group] = [
                jnp.dot(x, w_ref[:, columns(part)], preferred_element_type=F32).astype(BF16) for part in (1, 2)
            ]

    def lanes_of(pair):
        return slice(pair % inside * LANES, (pair % inside + 1) * LANES)

    def score(pair):
        if pair < pairs:
            project(pair // inside)
            scores[pair] = scores_of(query_of(pair), groups[pair // inside][0][:, lanes_of(pair)], bias)

    def weigh(pair, highest, weights):
        values2 = groups[pair // inside][1][:, lanes_of(pair)]
        beside = jnp.concatenate([values2, jnp.ones_like(values2)], axis=1)
        result = jnp.dot(weights, beside, preferred_element_type=F32)
        finish(pair, (merge(highest), merge(result[:, LANES:]), merge(result[:, :LANES])))

    score(0)
    waiting = None
    for pair in range(pairs):
        if (pair + 1) % inside == 1:
            project((pair + 1) // inside + 1)
        score(pair + 1)
        current = scores.pop(pair)
        highest = jnp.max(current, axis=-1, keepdims=True)
        weights = jnp.exp2((current - highest) * factor).astype(BF16)
        if waiting is not None:
            weigh(*waiting)
        waiting = (pair, highest, weights)
    weigh(*waiting)


def key_bias(here_ref, sources_ref, list_ref, count_ref, slots, sizes):
    lane = lax.broadcasted_iota(jnp.int32, (1, sum(sizes)), 1)
    bias = jnp.zeros((1, sum(sizes)), F32)
    count = count_ref[0, 0]
    start = 0
    for slot, size in zip(slots, sizes):
        if slot == OWN:
            start += size
            continue
        if slot == ABOVE:
            linked = here_ref[0]
        elif slot == BELOW:
            linked = here_ref[1]
        else:
            source = sources_ref[here_ref[3], slot]
            linked = jnp.int32(0)
            for entry in range(list_ref.shape[-1]):
                hit = (list_ref[0, 0, entry] == source) & (entry < count)
                linked = linked | hit.astype(jnp.int32)
        value = jnp.where(linked > 0, 0.0, MASKED).astype(F32)
        bias = jnp.where((lane >= start) & (lane < start + size), value, bias)
        start += size
    return bias


def joined(blocks):
    return blocks[0][...] if len(blocks) == 1 else jnp.concatenate([b[...] for b in blocks], axis=0)


def own_kernel(
    factor, slots, sizes, here_ref, sources_ref, list_ref, count_ref, x_ref, ahead_ref, behind_ref, w_ref,
    handed_ref, query_ref, high_ref, sum_ref, acc_ref,
):
    tokens, width = x_ref.shape
    x = x_ref[...]
    handed_ref[...] = x_ref[tokens - handed_ref.shape[0] :, :]
    bias = key_bias(here_ref, sources_ref, list_ref, count_ref, slots, sizes)
    low = lax.broadcasted_iota(jnp.int32, (tokens, LANES), 1) < LANES // 2
    zero = jnp.zeros((tokens, LANES), BF16)
    inside = GROUP // LANES
    queries = {}

    def query_of(pair):
        group = pair // inside
        if group not in queries:
            columns = slice(group * GROUP, (group + 1) * GROUP)
            queries[group] = jnp.dot(x, w_ref[:, columns], preferred_element_type=F32).astype(BF16)
        part = queries[group][:, pair % inside * LANES : (pair % inside + 1) * LANES]
        query2 = jnp.concatenate([jnp.where(low, part, zero), jnp.where(low, zero, part)], axis=0)
        query_ref[pair] = query2
        return query2

    def finish(pair, part):
        lanes = slice(pair * LANES, (pair + 1) * LANES)
        high_ref[:, lanes], sum_ref[:, lanes], acc_ref[:, lanes] = part

    seen = joined([x_ref, ahead_ref, behind_ref])
    attend_pairs(factor, seen, w_ref, bias, query_of, finish)


def combine(state, part, factor):
    high = jnp.maximum(state[0], part[0])
    old = jnp.exp2((state[0] - high) * factor)
    new = jnp.exp2((part[0] - high) * factor)
    return high, state[1] * old + part[1] * new, state[2] * old + part[2] * new


def batch_kernel(
    factor, slots, sizes, here_ref, sources_ref, list_ref, count_ref, query_ref, w_ref, high_in, sum_in, acc_in, edge_ref, *refs
):
    blocks, (high_ref, sum_ref, acc_ref, handed_ref) = refs[:-4], refs[-4:]
    handed_ref[...] = edge_ref[...]
    bias = key_bias(here_ref, sources_ref, list_ref, count_ref, slots, sizes)

    def finish(pair, part):
        lanes = slice(pair * LANES, (pair + 1) * LANES)
        state = combine((high_in[:, lanes], sum_in[:, lanes], acc_in[:, lanes]), part, factor)
        high_ref[:, lanes], sum_ref[:, lanes], acc_ref[:, lanes] = state

    attend_pairs(factor, joined(blocks), w_ref, bias, lambda pair: query_ref[pair], finish)


def last_kernel(
    factor, dims, slots, sizes, here_ref, sources_ref, list_ref, count_ref, query_ref, w_ref, high_in, sum_in, acc_in,
    wo_ref, inner_ref, edge_ref, *refs
):
    blocks, (dense, after_ref, north_ref, south_ref, across_ref, pair_ref, total) = refs[:-7], refs[-7:]
    levels, columns, rows = dims
    x = joined(blocks)
    width = x.shape[1]
    bias = key_bias(here_ref, sources_ref, list_ref, count_ref, slots, sizes)
    edge_at = inner_ref.shape[0]
    total[0:edge_at, :] = inner_ref[...].astype(F32)
    total[edge_at:, :] = edge_ref[...].astype(F32)

    def finish(pair, part):
        lanes = slice(pair * LANES, (pair + 1) * LANES)
        _, summed, result = combine((high_in[:, lanes], sum_in[:, lanes], acc_in[:, lanes]), part, factor)
        dense[:, lanes] = result / summed
        if (pair + 1) * LANES % GROUP == 0:
            chunk = slice((pair + 1) * LANES - GROUP, (pair + 1) * LANES)
            total[...] += jnp.dot(dense[:, chunk].astype(BF16), wo_ref[chunk, :], preferred_element_type=F32)

    attend_pairs(factor, x, w_ref, bias, lambda pair: query_ref[pair], finish)
    for index in range(width // LANES):
        lanes = slice(index * LANES, (index + 1) * LANES)
        after_ref[index] = total[:, lanes].astype(BF16).astype(F32)
        for out_ref, row in ((north_ref, 0), (south_ref, rows - 1)):
            pieces = []
            for level in range(levels):
                west_at = edge_at + level * 2 * rows + row
                inner = after_ref[index, pl.ds(level * (columns - 2) * rows + row, columns - 2, stride=rows), :]
                pieces += [after_ref[index, west_at : west_at + 1, :], inner]
                pieces += [after_ref[index, west_at + rows : west_at + rows + 1, :]]
            out_ref[:, lanes] = jnp.concatenate(pieces, axis=0).astype(BF16)
        sides = []
        for side in range(2):
            places = [edge_at + (level * 2 + side) * rows for level in range(levels)]
            sides.append(jnp.concatenate([after_ref[index, at : at + rows, :] for at in places], axis=0))
        across_ref[:, lanes] = jnp.where(here_ref[2] > 0, sides[0], sides[1]).astype(BF16)
        pair_ref[:, lanes] = jnp.where(here_ref[2] > 0, sides[1], sides[0]).astype(BF16)


def shape(dims, kind):
    return jax.ShapeDtypeStruct(dims, kind)


def call(kernel, out_shape, scalars, arrays, scratch, name, microseconds, outside=()):
    return pl.pallas_call(
        kernel,
        out_shape=out_shape,
        in_specs=[pl.BlockSpec(memory_space=pltpu.SMEM)] * len(scalars) + [pl.BlockSpec(memory_space=pltpu.VMEM)] * len(arrays)
        + [pl.BlockSpec(memory_space=pl.ANY)] * len(outside),
        out_specs=jax.tree.map(lambda _: pl.BlockSpec(memory_space=pltpu.VMEM), out_shape),
        scratch_shapes=scratch,
        compiler_params=pltpu.CompilerParams(vmem_limit_bytes=VMEM_LIMIT),
        cost_estimate=pl.CostEstimate(flops=int(microseconds * 1.1e9), bytes_accessed=0, transcendentals=0),
        name=name,
    )(*scalars, *arrays, *outside)


def swap(value, first):
    count = lax.axis_size("lon")
    pairs = [p for i in range(first, count, 2) for p in ((i, (i + 1) % count), ((i + 1) % count, i))]
    return lax.ppermute(value, "lon", pairs)


def exchange(north_edge, south_edge, across, pair, even, rows):
    across, pair = swap(across, 1), swap(pair, 0)
    even = even > 0
    west, east = jnp.where(even, across, pair), jnp.where(even, pair, across)

    def row(edge, at):
        return jnp.concatenate([edge, west[at::rows], east[at::rows]], axis=0)

    north = shift(row(south_edge, rows - 1), "lat", 1)
    south = shift(row(north_edge, 0), "lat", -1)
    return north, south, across, pair


def local(fields, conv_first, w_qkv, w_out, conv_second, key_list, key_count):
    fields = fields.transpose(0, 2, 1, 3)
    levels, columns, rows, width = fields.shape
    tokens = levels * rows * columns
    pairs = width // LANES
    factor = float(np.log2(np.e) * (width // HEADS) ** -0.5)
    lat_here = lax.axis_index("lat")
    lon_here = lax.axis_index("lon")
    lon_total = lax.axis_size("lon")
    order = ring_order(lon_total)
    place = {lon: i for i, lon in enumerate(order)}
    half = lon_total // 2
    table = np.zeros((lon_total, lon_total), np.int32)
    for lon in range(lon_total):
        for step in range(1, half + 1):
            table[lon, 2 * step - 2] = order[(place[lon] - step) % lon_total]
            table[lon, 2 * step - 1] = order[(place[lon] + step) % lon_total]
    here = jnp.stack(
        [lat_here > 0, lat_here < lax.axis_size("lat") - 1, lon_here % 2 == 0, lon_here]
    ).astype(jnp.int32)
    links = (here, jnp.asarray(table), key_list, key_count)

    dims = (levels, columns, rows)
    tiles = width // LANES
    edge_tokens = levels * 2 * rows
    inner_tokens = tokens - edge_tokens
    full = lambda count: pltpu.VMEM((tiles, count, LANES), F32)
    flat = lambda count: shape((count, width), BF16)
    part_shape = (shape((tiles, tokens, LANES), F32), shape((tiles, 9, LANES), F32))
    tall = flat(levels * (rows + 2))
    forward = [(order[i], order[(i + 1) % lon_total]) for i in range(lon_total)]
    backward = [(b, a) for a, b in forward]

    edge_rows = flat(levels * columns)
    near = shape(fields.shape, BF16)
    north_edge, south_edge, fields = call(
        rows_kernel, (edge_rows, edge_rows, near), (), (fields,), [full(tokens)], "edge_rows", 1
    )
    north = shift(south_edge, "lat", 1)
    south = shift(north_edge, "lat", -1)
    part = call(first_part_kernel, part_shape, (), (fields, conv_first), [], "conv_part", 1)
    stream_inner, normed_inner, across, pair, even = call(
        functools.partial(inner_kernel, dims),
        (flat(inner_tokens), flat(inner_tokens), tall, tall, shape((1, width), jnp.int32)),
        (here,),
        (*part, north, south, fields),
        [full(inner_tokens)],
        "conv_inner",
        1,
    )
    ahead = lax.ppermute(normed_inner, "lon", forward)
    behind = lax.ppermute(normed_inner, "lon", backward)
    across, pair = swap(across, 1), swap(pair, 0)
    anywhere = pl.BlockSpec(memory_space=pl.ANY)
    vmem = pl.BlockSpec(memory_space=pltpu.VMEM)
    inner_passed, w_qkv = pl.pallas_call(
        weights_kernel,
        out_shape=(flat(inner_tokens), shape(w_qkv.shape, BF16)),
        in_specs=[vmem, anywhere],
        out_specs=(vmem, vmem),
        scratch_shapes=[pltpu.SemaphoreType.DMA],
        compiler_params=pltpu.CompilerParams(vmem_limit_bytes=VMEM_LIMIT),
        cost_estimate=pl.CostEstimate(flops=int(2e9), bytes_accessed=0, transcendentals=0),
        name="weights_near",
    )(normed_inner, w_qkv)
    stream_edge, normed_edge, normed, *both = call(
        functools.partial(edge_kernel, dims),
        (flat(edge_tokens), flat(edge_tokens), flat(tokens), flat(tokens), flat(tokens)),
        (here,),
        (*part, north, south, across, pair, normed_inner, ahead, behind),
        [full(edge_tokens)],
        "conv_edge",
        1,
    )

    state_shape = (shape((tokens, width), F32),) * 3
    edge_passed, query, *state = call(
        functools.partial(own_kernel, factor, [OWN, 0, 1], [tokens, inner_tokens, inner_tokens]),
        (flat(edge_tokens), shape((pairs, 2 * tokens, LANES), BF16), *state_shape),
        links,
        (normed, ahead, behind, w_qkv),
        [],
        "own_block",
        4,
    )

    def batch(state, waiting):
        blocks = [block for block, _ in waiting]
        slots, sizes = zip(*[piece for _, pieces in waiting for piece in pieces])
        *state, handed = call(
            functools.partial(batch_kernel, factor, slots, sizes),
            (*state_shape, flat(edge_tokens)),
            links,
            (query, w_qkv, *state, normed_edge, *blocks),
            [],
            "attend_batch",
            1 + 1.2 * len(blocks),
        )
        return state, handed

    sides = ((ABOVE, 1), (BELOW, -1))
    near = {
        2: [(shift(inner_passed, "lat", by), [(slot, inner_tokens)]) for slot, by in sides],
        3: [(shift(edge_passed, "lat", by), [(slot, edge_tokens)]) for slot, by in sides],
    }
    ahead, behind = both
    for step in range(2, half):
        ahead = lax.ppermute(ahead, "lon", forward)
        behind = lax.ppermute(behind, "lon", backward)
        if step > 2:
            state, handed = batch(state, waiting)
            if step == 3:
                opposite = [(order[i], order[(i + half) % lon_total]) for i in range(lon_total)]
                far_edge = lax.ppermute(handed, "lon", opposite)
        waiting = [
            (ahead, [(2 * step - 2, inner_tokens), (2 * step - 4, edge_tokens)]),
            (behind, [(2 * step - 1, inner_tokens), (2 * step - 3, edge_tokens)]),
            *near.get(step, ()),
        ]
    last = lon_total - 2
    cut = (inner_tokens + 31) // 32 * 16
    far_first = lax.ppermute(jnp.concatenate([ahead[:cut], ahead[inner_tokens:]]), "lon", forward)
    far_second = lax.ppermute(behind[cut:], "lon", backward)
    state, _ = batch(state, waiting)
    slots = [last, last - 2, last, last - 1, last]
    sizes = [cut, edge_tokens, inner_tokens - cut, edge_tokens, edge_tokens]

    row_edge, column_edge = flat(levels * columns), flat(levels * rows)
    dense, after, *edges = call(
        functools.partial(last_kernel, factor, dims, slots, sizes),
        (shape((tokens, width), F32), part_shape[0], row_edge, row_edge, column_edge, column_edge),
        links,
        (query, w_qkv, *state, w_out, stream_inner, stream_edge, far_first, far_second, far_edge),
        [pltpu.VMEM((tokens, width), F32)],
        "attend_last",
        5,
    )
    north, south, across, pair = exchange(*edges, even, rows)
    grid4 = shape(fields.shape, BF16)
    *part, attended = call(
        functools.partial(second_part_kernel, dims),
        (*part_shape, grid4),
        (here,),
        (after, conv_second, dense, across, pair),
        [],
        "conv_part",
        2,
    )
    mixed = call(functools.partial(second_kernel, dims), grid4, (here,), (*part, north, south), [full(tokens)], "conv_second", 2)
    return attended.transpose(0, 2, 1, 3), mixed.transpose(0, 2, 1, 3)


def solution(mesh):
    return jax.shard_map(
        local,
        mesh=mesh,
        in_specs=(
            P(None, "lat", "lon", None),
            P(),
            P(),
            P(),
            P(),
            P("lat", "lon", None),
            P("lat", "lon"),
        ),
        out_specs=(P(None, "lat", "lon", None), P(None, "lat", "lon", None)),
        check_vma=False,
    )
```

```python
import functools

import jax
import jax.numpy as jnp
import numpy as np
from jax import lax
from jax.experimental import pallas as pl
from jax.experimental.pallas import tpu as pltpu
from jax.sharding import PartitionSpec as P

HEADS = 16
EPSILON = 1e-05
MASKED = -1e30
LANES = 128
SUBLANES = 8
GROUP = 256
F32 = jnp.float32
BF16 = jnp.bfloat16
VMEM_LIMIT = 16 * 1024 * 1024
ABOVE, BELOW, OWN = -1, -2, -3


def ring_order(count):
    columns = 1
    while columns * columns * 4 <= count:
        columns *= 2
    rows = count // columns
    order = [z * columns for z in range(rows)]
    for turn, z in enumerate(range(rows - 1, -1, -1)):
        ys = list(range(1, columns))
        if turn % 2:
            ys.reverse()
        order += [z * columns + y for y in ys]
    return order


def shift(x, axis, by):
    size = lax.axis_size(axis)
    return lax.ppermute(x, axis, [(i, (i + by) % size) for i in range(size)])


def place(dims, level, column):
    levels, columns, rows = dims
    inner = columns - 2
    if 0 < column <= inner:
        return (level * inner + column - 1) * rows
    return (levels * inner + level * 2 + (column > 0)) * rows


def conv_part(load, dims, weights_ref, part_ref, taps_ref):
    levels, columns, rows = dims
    above = lax.broadcasted_iota(jnp.int32, (SUBLANES, LANES), 0) > 0
    blank = jnp.zeros((SUBLANES - rows, LANES), F32)
    nothing = jnp.zeros((SUBLANES, LANES), F32)

    def tile(index, carry):
        lanes = pl.ds(pl.multiple_of(index * LANES, LANES), LANES)
        taps_ref[index] = weights_ref[:, lanes]
        taps = [jnp.broadcast_to(weights_ref[k : k + 1, lanes], (SUBLANES, LANES)) for k in range(9)]
        for level in range(levels):
            strip = [jnp.concatenate([load(level, column, index, lanes), blank], axis=0) for column in range(columns)]
            strip = [nothing, *strip, nothing]
            for column in range(columns):
                near = strip[column : column + 3]
                sums = [taps[3 * a] * near[0] + taps[3 * a + 1] * near[1] + taps[3 * a + 2] * near[2] for a in range(3)]
                value = near[1] + sums[1]
                value += jnp.where(above, pltpu.roll(sums[0], 1, 0), 0.0)
                value += pltpu.roll(sums[2], SUBLANES - 1, 0)
                at = place(dims, level, column)
                part_ref[index, at : at + rows, :] = value[0:rows]
        return carry

    lax.fori_loop(0, part_ref.shape[0], tile, 0)


def rows_kernel(field_ref, north_ref, south_ref, near_ref, flat_ref):
    near_ref[...] = field_ref[...]
    levels, columns, rows, width = field_ref.shape
    count = levels * columns
    for index in range(width // LANES):
        lanes = slice(index * LANES, (index + 1) * LANES)
        for level in range(levels):
            for column in range(columns):
                at = (level * columns + column) * rows
                flat_ref[index, at : at + rows, :] = field_ref[level, column, :, lanes].astype(F32)
        north_ref[:, lanes] = flat_ref[index, pl.ds(0, count, stride=rows), :].astype(BF16)
        south_ref[:, lanes] = flat_ref[index, pl.ds(rows - 1, count, stride=rows), :].astype(BF16)


def first_part_kernel(field_ref, weights_ref, part_ref, taps_ref):
    levels, columns, rows, _ = field_ref.shape
    load = lambda level, column, index, lanes: field_ref[level, column, :, lanes].astype(F32)
    conv_part(load, (levels, columns, rows), weights_ref, part_ref, taps_ref)


def weights_kernel(inner_ref, far_ref, passed_ref, near_ref, arrived):
    copy = pltpu.make_async_copy(far_ref, near_ref, arrived)
    copy.start()
    passed_ref[...] = inner_ref[...]
    copy.wait()


def second_part_kernel(
    dims, here_ref, field_ref, weights_ref, dense_ref, across_ref, pair_ref, part_ref, taps_ref, attended_ref
):
    levels, columns, rows = dims

    def load(level, column, index, lanes):
        at = place(dims, level, column)
        return field_ref[index, at : at + rows, :]

    conv_part(load, dims, weights_ref, part_ref, taps_ref)
    for index in range(part_ref.shape[0]):
        add_sides(index, dims, here_ref, across_ref, pair_ref, taps_ref, part_ref, levels * (columns - 2) * rows)
    for level in range(levels):
        for column in range(columns):
            at = place(dims, level, column)
            attended_ref[level, column] = dense_ref[at : at + rows, :].astype(BF16)


def add_rows(index, dims, here_ref, north_ref, south_ref, taps_ref, full, inner_at, edge_at):
    levels, columns, rows = dims
    inner = columns - 2
    lanes = slice(index * LANES, (index + 1) * LANES)
    blank = jnp.zeros((1, LANES), F32)
    count = levels * columns
    for ref, flag, a, row in ((north_ref, 0, 0, 0), (south_ref, 1, 2, rows - 1)):
        lines = ref[:, lanes].astype(F32)
        for level in range(levels):
            ends = [blank, blank]
            if lines.shape[0] > count:
                ends = [lines[at : at + 1] for at in (count + level, count + levels + level)]
            line = jnp.concatenate([ends[0], lines[level * columns : (level + 1) * columns], ends[1]], axis=0)
            left, line, right = (line[b : b + columns] for b in range(3))
            tap = [taps_ref[index, 3 * a + b : 3 * a + b + 1, :] for b in range(3)]
            more = tap[0] * left + tap[1] * line + tap[2] * right
            more = jnp.where(here_ref[flag] > 0, more, 0.0)
            if inner_at is not None:
                full[index, pl.ds(inner_at + level * inner * rows + row, inner, stride=rows), :] += more[1 : columns - 1]
            if edge_at is not None:
                ends = jnp.concatenate([more[:1], more[columns - 1 :]], axis=0)
                full[index, pl.ds(edge_at + level * 2 * rows + row, 2, stride=rows), :] += ends


def add_sides(index, dims, here_ref, across_ref, pair_ref, taps_ref, full, edge_at):
    levels, columns, rows = dims
    lanes = slice(index * LANES, (index + 1) * LANES)
    even = here_ref[2] > 0
    blank = jnp.zeros((1, LANES), F32)
    pair = pair_ref[:, lanes].astype(F32)
    across = across_ref[:, lanes].astype(F32)
    both = jnp.where(even, across, pair), jnp.where(even, pair, across)
    tall = pair.shape[0] // levels
    for level in range(levels):
        west, east = (side[level * tall : (level + 1) * tall] for side in both)
        for side, b, order in ((west, 0, 0), (east, 2, 1)):
            if side.shape[0] == rows:
                side = jnp.concatenate([blank, side, blank], axis=0)
            more = None
            for a in range(3):
                term = taps_ref[index, 3 * a + b : 3 * a + b + 1, :] * side[a : a + rows]
                more = term if more is None else more + term
            at = edge_at + (level * 2 + order) * rows
            full[index, at : at + rows, :] += more


def normalise(full, stream_ref, put):
    tiles, tokens, _ = full.shape
    squares = jnp.zeros((tokens, LANES), F32)
    for index in range(tiles):
        stream = full[index].astype(BF16)
        stream_ref[:, index * LANES : (index + 1) * LANES] = stream
        wide = stream.astype(F32)
        squares += wide * wide
    mean = jnp.sum(squares, axis=-1, keepdims=True) * (1.0 / (tiles * LANES))
    scale = jnp.broadcast_to(lax.rsqrt(mean + EPSILON), (tokens, LANES))
    for index in range(tiles):
        lanes = slice(index * LANES, (index + 1) * LANES)
        put(lanes, (stream_ref[:, lanes].astype(F32) * scale).astype(BF16))


def inner_kernel(
    dims, here_ref, part_ref, taps_ref, north_ref, south_ref, field_ref,
    stream_ref, normed_ref, across_ref, pair_ref, even_ref, full,
):
    levels, columns, rows = dims
    tiles, tokens, _ = full.shape
    for index in range(tiles):
        full[index] = part_ref[index, 0:tokens, :]
        add_rows(index, dims, here_ref, north_ref, south_ref, taps_ref, full, 0, None)

    def put(lanes, value):
        normed_ref[:, lanes] = value

    normalise(full, stream_ref, put)
    even_ref[...] = jnp.full(even_ref.shape, here_ref[2], jnp.int32)
    has_north = (here_ref[0] > 0).astype(F32)
    has_south = (here_ref[1] > 0).astype(F32)
    even = here_ref[2] > 0
    north = north_ref[...].astype(F32) * has_north
    south = south_ref[...].astype(F32) * has_south
    tall = []
    for column in (0, columns - 1):
        pieces = []
        for level in range(levels):
            at = level * columns + column
            pieces += [north[at : at + 1], field_ref[level, column].astype(F32), south[at : at + 1]]
        tall.append(jnp.concatenate(pieces, axis=0))
    across_ref[...] = jnp.where(even, tall[0], tall[1]).astype(BF16)
    pair_ref[...] = jnp.where(even, tall[1], tall[0]).astype(BF16)


def edge_kernel(
    dims, here_ref, part_ref, taps_ref, north_ref, south_ref, across_ref, pair_ref, inner_ref, ahead_ref, behind_ref,
    stream_ref, edge_ref, normed_ref, ahead_joined, behind_joined, full,
):
    tiles, tokens, _ = full.shape
    start = part_ref.shape[1] - tokens
    normed_ref[0:start, :] = inner_ref[...]
    ahead_joined[0:start, :] = ahead_ref[...]
    behind_joined[0:start, :] = behind_ref[...]
    for index in range(tiles):
        full[index] = part_ref[index, start : start + tokens, :]
        add_rows(index, dims, here_ref, north_ref, south_ref, taps_ref, full, None, 0)
        add_sides(index, dims, here_ref, across_ref, pair_ref, taps_ref, full, 0)

    def put(lanes, value):
        edge_ref[:, lanes] = value
        for ref in (normed_ref, ahead_joined, behind_joined):
            ref[start : start + tokens, lanes] = value

    normalise(full, stream_ref, put)


def second_kernel(dims, here_ref, part_ref, taps_ref, north_ref, south_ref, mixed_ref, full, near_ref, sent):
    levels, columns, rows = dims
    edge_at = levels * (columns - 2) * rows
    tiles = part_ref.shape[0]
    for index in range(tiles):
        full[index] = part_ref[index]
        add_rows(index, dims, here_ref, north_ref, south_ref, taps_ref, full, 0, edge_at)
    copies = []
    for level in range(levels):
        for index in range(tiles):
            lanes = slice(index * LANES, (index + 1) * LANES)
            for column in range(columns):
                at = place(dims, level, column)
                near_ref[level, column, :, lanes] = full[index, at : at + rows, :].astype(BF16)
        copies.append(pltpu.make_async_copy(near_ref.at[level], mixed_ref.at[level], sent.at[level]))
        copies[-1].start()
    for copy in copies:
        copy.wait()


def scores_of(query2, keys2, bias):
    scores = lax.dot_general(query2, keys2, (((1,), (1,)), ((), ())), preferred_element_type=F32)
    return scores if bias is None else scores + bias


def merge(both):
    half = both.shape[0] // 2
    low = lax.broadcasted_iota(jnp.int32, (half, LANES), 1) < LANES // 2
    return jnp.where(low, both[:half], both[half:])


def attend_pairs(factor, x, w_ref, bias, query_of, finish):
    width = x.shape[1]
    pairs = width // LANES
    inside = GROUP // LANES
    groups, scores = {}, {}

    def project(group):
        if group * GROUP < width and group not in groups:
            columns = lambda part: slice(part * width + group * GROUP, part * width + (group + 1) * GROUP)
            groups[group] = [
                jnp.dot(x, w_ref[:, columns(part)], preferred_element_type=F32).astype(BF16) for part in (1, 2)
            ]

    def lanes_of(pair):
        return slice(pair % inside * LANES, (pair % inside + 1) * LANES)

    def score(pair):
        if pair < pairs:
            project(pair // inside)
            scores[pair] = scores_of(query_of(pair), groups[pair // inside][0][:, lanes_of(pair)], bias)

    def weigh(pair, highest, weights):
        values2 = groups[pair // inside][1][:, lanes_of(pair)]
        beside = jnp.concatenate([values2, jnp.ones_like(values2)], axis=1)
        result = jnp.dot(weights, beside, preferred_element_type=F32)
        finish(pair, (merge(highest), merge(result[:, LANES:]), merge(result[:, :LANES])))

    score(0)
    waiting = None
    for pair in range(pairs):
        if (pair + 1) % inside == 1:
            project((pair + 1) // inside + 1)
        score(pair + 1)
        current = scores.pop(pair)
        highest = jnp.max(current, axis=-1, keepdims=True)
        weights = jnp.exp2((current - highest) * factor).astype(BF16)
        if waiting is not None:
            weigh(*waiting)
        waiting = (pair, highest, weights)
    weigh(*waiting)


def key_bias(here_ref, sources_ref, list_ref, count_ref, slots, sizes):
    lane = lax.broadcasted_iota(jnp.int32, (1, sum(sizes)), 1)
    bias = jnp.zeros((1, sum(sizes)), F32)
    count = count_ref[0, 0]
    start = 0
    for slot, size in zip(slots, sizes):
        if slot == OWN:
            start += size
            continue
        if slot == ABOVE:
            linked = here_ref[0]
        elif slot == BELOW:
            linked = here_ref[1]
        else:
            source = sources_ref[here_ref[3], slot]
            linked = jnp.int32(0)
            for entry in range(list_ref.shape[-1]):
                hit = (list_ref[0, 0, entry] == source) & (entry < count)
                linked = linked | hit.astype(jnp.int32)
        value = jnp.where(linked > 0, 0.0, MASKED).astype(F32)
        bias = jnp.where((lane >= start) & (lane < start + size), value, bias)
        start += size
    return bias


def joined(blocks):
    return blocks[0][...] if len(blocks) == 1 else jnp.concatenate([b[...] for b in blocks], axis=0)


def own_kernel(
    factor, slots, sizes, here_ref, sources_ref, list_ref, count_ref, x_ref, ahead_ref, behind_ref, w_ref,
    handed_ref, query_ref, high_ref, sum_ref, acc_ref,
):
    tokens, width = x_ref.shape
    x = x_ref[...]
    handed_ref[...] = x_ref[tokens - handed_ref.shape[0] :, :]
    bias = key_bias(here_ref, sources_ref, list_ref, count_ref, slots, sizes)
    low = lax.broadcasted_iota(jnp.int32, (tokens, LANES), 1) < LANES // 2
    zero = jnp.zeros((tokens, LANES), BF16)
    inside = GROUP // LANES
    queries = {}

    def query_of(pair):
        group = pair // inside
        if group not in queries:
            columns = slice(group * GROUP, (group + 1) * GROUP)
            queries[group] = jnp.dot(x, w_ref[:, columns], preferred_element_type=F32).astype(BF16)
        part = queries[group][:, pair % inside * LANES : (pair % inside + 1) * LANES]
        query2 = jnp.concatenate([jnp.where(low, part, zero), jnp.where(low, zero, part)], axis=0)
        query_ref[pair] = query2
        return query2

    def finish(pair, part):
        lanes = slice(pair * LANES, (pair + 1) * LANES)
        high_ref[:, lanes], sum_ref[:, lanes], acc_ref[:, lanes] = part

    seen = joined([x_ref, ahead_ref, behind_ref])
    attend_pairs(factor, seen, w_ref, bias, query_of, finish)


def combine(state, part, factor):
    high = jnp.maximum(state[0], part[0])
    old = jnp.exp2((state[0] - high) * factor)
    new = jnp.exp2((part[0] - high) * factor)
    return high, state[1] * old + part[1] * new, state[2] * old + part[2] * new


def batch_kernel(
    factor, slots, sizes, here_ref, sources_ref, list_ref, count_ref, query_ref, w_ref, high_in, sum_in, acc_in, edge_ref, *refs
):
    blocks, (high_ref, sum_ref, acc_ref, handed_ref) = refs[:-4], refs[-4:]
    handed_ref[...] = edge_ref[...]
    bias = key_bias(here_ref, sources_ref, list_ref, count_ref, slots, sizes)

    def finish(pair, part):
        lanes = slice(pair * LANES, (pair + 1) * LANES)
        state = combine((high_in[:, lanes], sum_in[:, lanes], acc_in[:, lanes]), part, factor)
        high_ref[:, lanes], sum_ref[:, lanes], acc_ref[:, lanes] = state

    attend_pairs(factor, joined(blocks), w_ref, bias, lambda pair: query_ref[pair], finish)


def last_kernel(
    factor, dims, slots, sizes, here_ref, sources_ref, list_ref, count_ref, query_ref, w_ref, high_in, sum_in, acc_in,
    wo_ref, inner_ref, edge_ref, *refs
):
    blocks, (dense, after_ref, north_ref, south_ref, across_ref, pair_ref, total) = refs[:-7], refs[-7:]
    levels, columns, rows = dims
    x = joined(blocks)
    width = x.shape[1]
    bias = key_bias(here_ref, sources_ref, list_ref, count_ref, slots, sizes)
    edge_at = inner_ref.shape[0]
    total[0:edge_at, :] = inner_ref[...].astype(F32)
    total[edge_at:, :] = edge_ref[...].astype(F32)

    def finish(pair, part):
        lanes = slice(pair * LANES, (pair + 1) * LANES)
        _, summed, result = combine((high_in[:, lanes], sum_in[:, lanes], acc_in[:, lanes]), part, factor)
        dense[:, lanes] = result / summed
        if (pair + 1) * LANES % GROUP == 0:
            chunk = slice((pair + 1) * LANES - GROUP, (pair + 1) * LANES)
            total[...] += jnp.dot(dense[:, chunk].astype(BF16), wo_ref[chunk, :], preferred_element_type=F32)

    attend_pairs(factor, x, w_ref, bias, lambda pair: query_ref[pair], finish)
    for index in range(width // LANES):
        lanes = slice(index * LANES, (index + 1) * LANES)
        after_ref[index] = total[:, lanes].astype(BF16).astype(F32)
        for out_ref, row in ((north_ref, 0), (south_ref, rows - 1)):
            pieces = []
            for level in range(levels):
                west_at = edge_at + level * 2 * rows + row
                inner = after_ref[index, pl.ds(level * (columns - 2) * rows + row, columns - 2, stride=rows), :]
                pieces += [after_ref[index, west_at : west_at + 1, :], inner]
                pieces += [after_ref[index, west_at + rows : west_at + rows + 1, :]]
            out_ref[:, lanes] = jnp.concatenate(pieces, axis=0).astype(BF16)
        sides = []
        for side in range(2):
            places = [edge_at + (level * 2 + side) * rows for level in range(levels)]
            sides.append(jnp.concatenate([after_ref[index, at : at + rows, :] for at in places], axis=0))
        across_ref[:, lanes] = jnp.where(here_ref[2] > 0, sides[0], sides[1]).astype(BF16)
        pair_ref[:, lanes] = jnp.where(here_ref[2] > 0, sides[1], sides[0]).astype(BF16)


def shape(dims, kind):
    return jax.ShapeDtypeStruct(dims, kind)


def call(kernel, out_shape, scalars, arrays, scratch, name, microseconds, outside=()):
    return pl.pallas_call(
        kernel,
        out_shape=out_shape,
        in_specs=[pl.BlockSpec(memory_space=pltpu.SMEM)] * len(scalars) + [pl.BlockSpec(memory_space=pltpu.VMEM)] * len(arrays)
        + [pl.BlockSpec(memory_space=pl.ANY)] * len(outside),
        out_specs=jax.tree.map(lambda _: pl.BlockSpec(memory_space=pltpu.VMEM), out_shape),
        scratch_shapes=scratch,
        compiler_params=pltpu.CompilerParams(vmem_limit_bytes=VMEM_LIMIT),
        cost_estimate=pl.CostEstimate(flops=int(microseconds * 1.1e9), bytes_accessed=0, transcendentals=0),
        name=name,
    )(*scalars, *arrays, *outside)


def swap(value, first):
    count = lax.axis_size("lon")
    pairs = [p for i in range(first, count, 2) for p in ((i, (i + 1) % count), ((i + 1) % count, i))]
    return lax.ppermute(value, "lon", pairs)


def exchange(north_edge, south_edge, across, pair, even, rows):
    across, pair = swap(across, 1), swap(pair, 0)
    even = even > 0
    west, east = jnp.where(even, across, pair), jnp.where(even, pair, across)

    def row(edge, at):
        return jnp.concatenate([edge, west[at::rows], east[at::rows]], axis=0)

    north = shift(row(south_edge, rows - 1), "lat", 1)
    south = shift(row(north_edge, 0), "lat", -1)
    return north, south, across, pair


def local(fields, conv_first, w_qkv, w_out, conv_second, key_list, key_count):
    fields = fields.transpose(0, 2, 1, 3)
    levels, columns, rows, width = fields.shape
    tokens = levels * rows * columns
    pairs = width // LANES
    factor = float(np.log2(np.e) * (width // HEADS) ** -0.5)
    lat_here = lax.axis_index("lat")
    lon_here = lax.axis_index("lon")
    lon_total = lax.axis_size("lon")
    order = ring_order(lon_total)
    place = {lon: i for i, lon in enumerate(order)}
    half = lon_total // 2
    table = np.zeros((lon_total, lon_total), np.int32)
    for lon in range(lon_total):
        for step in range(1, half + 1):
            table[lon, 2 * step - 2] = order[(place[lon] - step) % lon_total]
            table[lon, 2 * step - 1] = order[(place[lon] + step) % lon_total]
    here = jnp.stack(
        [lat_here > 0, lat_here < lax.axis_size("lat") - 1, lon_here % 2 == 0, lon_here]
    ).astype(jnp.int32)
    links = (here, jnp.asarray(table), key_list, key_count)

    dims = (levels, columns, rows)
    tiles = width // LANES
    edge_tokens = levels * 2 * rows
    inner_tokens = tokens - edge_tokens
    full = lambda count: pltpu.VMEM((tiles, count, LANES), F32)
    flat = lambda count: shape((count, width), BF16)
    part_shape = (shape((tiles, tokens, LANES), F32), shape((tiles, 9, LANES), F32))
    tall = flat(levels * (rows + 2))
    forward = [(order[i], order[(i + 1) % lon_total]) for i in range(lon_total)]
    backward = [(b, a) for a, b in forward]

    edge_rows = flat(levels * columns)
    near = shape(fields.shape, BF16)
    north_edge, south_edge, fields = call(
        rows_kernel, (edge_rows, edge_rows, near), (), (fields,), [full(tokens)], "edge_rows", 1
    )
    north = shift(south_edge, "lat", 1)
    south = shift(north_edge, "lat", -1)
    part = call(first_part_kernel, part_shape, (), (fields, conv_first), [], "conv_part", 1)
    stream_inner, normed_inner, across, pair, even = call(
        functools.partial(inner_kernel, dims),
        (flat(inner_tokens), flat(inner_tokens), tall, tall, shape((1, width), jnp.int32)),
        (here,),
        (*part, north, south, fields),
        [full(inner_tokens)],
        "conv_inner",
        1,
    )
    ahead = lax.ppermute(normed_inner, "lon", forward)
    behind = lax.ppermute(normed_inner, "lon", backward)
    across, pair = swap(across, 1), swap(pair, 0)
    anywhere = pl.BlockSpec(memory_space=pl.ANY)
    vmem = pl.BlockSpec(memory_space=pltpu.VMEM)
    inner_passed, w_qkv = pl.pallas_call(
        weights_kernel,
        out_shape=(flat(inner_tokens), shape(w_qkv.shape, BF16)),
        in_specs=[vmem, anywhere],
        out_specs=(vmem, vmem),
        scratch_shapes=[pltpu.SemaphoreType.DMA],
        compiler_params=pltpu.CompilerParams(vmem_limit_bytes=VMEM_LIMIT),
        cost_estimate=pl.CostEstimate(flops=int(2e9), bytes_accessed=0, transcendentals=0),
        name="weights_near",
    )(normed_inner, w_qkv)
    stream_edge, normed_edge, normed, *both = call(
        functools.partial(edge_kernel, dims),
        (flat(edge_tokens), flat(edge_tokens), flat(tokens), flat(tokens), flat(tokens)),
        (here,),
        (*part, north, south, across, pair, normed_inner, ahead, behind),
        [full(edge_tokens)],
        "conv_edge",
        1,
    )

    state_shape = (shape((tokens, width), F32),) * 3
    edge_passed, query, *state = call(
        functools.partial(own_kernel, factor, [OWN, 0, 1], [tokens, inner_tokens, inner_tokens]),
        (flat(edge_tokens), shape((pairs, 2 * tokens, LANES), BF16), *state_shape),
        links,
        (normed, ahead, behind, w_qkv),
        [],
        "own_block",
        4,
    )

    def batch(state, waiting):
        blocks = [block for block, _ in waiting]
        slots, sizes = zip(*[piece for _, pieces in waiting for piece in pieces])
        *state, handed = call(
            functools.partial(batch_kernel, factor, slots, sizes),
            (*state_shape, flat(edge_tokens)),
            links,
            (query, w_qkv, *state, normed_edge, *blocks),
            [],
            "attend_batch",
            1 + 1.2 * len(blocks),
        )
        return state, handed

    sides = ((ABOVE, 1), (BELOW, -1))
    near = {
        2: [(shift(inner_passed, "lat", by), [(slot, inner_tokens)]) for slot, by in sides],
        3: [(shift(edge_passed, "lat", by), [(slot, edge_tokens)]) for slot, by in sides],
    }
    ahead, behind = both
    for step in range(2, half):
        ahead = lax.ppermute(ahead, "lon", forward)
        behind = lax.ppermute(behind, "lon", backward)
        if step > 2:
            state, handed = batch(state, waiting)
            if step == 3:
                opposite = [(order[i], order[(i + half) % lon_total]) for i in range(lon_total)]
                far_edge = lax.ppermute(handed, "lon", opposite)
        waiting = [
            (ahead, [(2 * step - 2, inner_tokens), (2 * step - 4, edge_tokens)]),
            (behind, [(2 * step - 1, inner_tokens), (2 * step - 3, edge_tokens)]),
            *near.get(step, ()),
        ]
    last = lon_total - 2
    cut = (inner_tokens + 31) // 32 * 16
    far_first = lax.ppermute(jnp.concatenate([ahead[:cut], ahead[inner_tokens:]]), "lon", forward)
    far_second = lax.ppermute(behind[cut:], "lon", backward)
    state, _ = batch(state, waiting)
    slots = [last, last - 2, last, last - 1, last]
    sizes = [cut, edge_tokens, inner_tokens - cut, edge_tokens, edge_tokens]

    row_edge, column_edge = flat(levels * columns), flat(levels * rows)
    dense, after, *edges = call(
        functools.partial(last_kernel, factor, dims, slots, sizes),
        (shape((tokens, width), F32), part_shape[0], row_edge, row_edge, column_edge, column_edge),
        links,
        (query, w_qkv, *state, w_out, stream_inner, stream_edge, far_first, far_second, far_edge),
        [pltpu.VMEM((tokens, width), F32)],
        "attend_last",
        5,
    )
    north, south, across, pair = exchange(*edges, even, rows)
    grid4 = shape(fields.shape, BF16)
    *part, attended = call(
        functools.partial(second_part_kernel, dims),
        (*part_shape, grid4),
        (here,),
        (after, conv_second, dense, across, pair),
        [],
        "conv_part",
        2,
    )
    vmem = pl.BlockSpec(memory_space=pltpu.VMEM)
    mixed = pl.pallas_call(
        functools.partial(second_kernel, dims),
        out_shape=grid4,
        in_specs=[pl.BlockSpec(memory_space=pltpu.SMEM)] + [vmem] * 4,
        out_specs=pl.BlockSpec(memory_space=pl.ANY),
        scratch_shapes=[full(tokens), pltpu.VMEM(grid4.shape, BF16), pltpu.SemaphoreType.DMA((levels,))],
        compiler_params=pltpu.CompilerParams(vmem_limit_bytes=VMEM_LIMIT),
        cost_estimate=pl.CostEstimate(flops=int(2e9), bytes_accessed=0, transcendentals=0),
        name="conv_second",
    )(here, *part, north, south)
    return attended.transpose(0, 2, 1, 3), mixed.transpose(0, 2, 1, 3)


def solution(mesh):
    return jax.shard_map(
        local,
        mesh=mesh,
        in_specs=(
            P(None, "lat", "lon", None),
            P(),
            P(),
            P(),
            P(),
            P("lat", "lon", None),
            P("lat", "lon"),
        ),
        out_specs=(P(None, "lat", "lon", None), P(None, "lat", "lon", None)),
        check_vma=False,
    )
```
